32 devices in a mesh: dp: 8 (over z, y), sp: 4 (over x, core).
Axes of the slice: x: 2, y: 2, z: 4, core: 2. Of those that a mesh axis runs over, the one named last changes fastest.
Arguments:
- queries: bfloat16 [4096, 3584], P(('dp', 'sp')), may hold values from -128 to 128
- keys: bfloat16 [4096, 512], P(('dp', 'sp')), may hold values from -6 to 6
- values: bfloat16 [4096, 512], P(('dp', 'sp')), may hold values from -6 to 6
- document_lengths: int32 [8, 8], P('dp'), may hold values from 1 to 256, 512 in all within a row
- pair_ids: int32 [64], P('dp'), may hold values from 0 to 63, as said below
Outputs:
- embeddings: bfloat16 [64, 3584], P('dp', 'sp')
- grads: float32 [64, 3584], P('dp', 'sp')
The draws below stay inside these ranges and needn't reach their ends.
Inputs may be any that keep to these rules, and one draw needn't show every extreme that they name: `document_lengths`: each row's 8 lengths sum to 512; the longest is exactly 256. pair_ids pairs the 64 documents two by two: pair_ids[pair_ids[i]] = i and pair_ids[i] != i.
All inputs are finite; a program needn't handle non-finite values.
Results may differ from the reference program's by a relative error of at most 0.0055.
Values may be sent and summed in bfloat16 or wider, within the bound.
No kernel may reach another device: no remote copies, remote signals or barrier semaphores. Data moves between devices by JAX's collectives and lax.ppermute only.
A program may use at most 64 MiB of HBM per device.

```python
import math
import jax
import jax.numpy as jnp
import numpy as np
from jax import lax

QUERY_HEADS = 28
KEY_VALUE_HEADS = 4
HEAD_SIZE = 128
DOCS = 8
WINDOW_TOKENS = 512
LONGEST = 256
NDOC = 64
BATCH_TOKENS = 4096
N_DP = 8


def key_field(key):
    return jnp.clip(jax.random.normal(key, (BATCH_TOKENS, KEY_VALUE_HEADS, HEAD_SIZE), jnp.float32), -6.0, 6.0)


def draw_keys(key, part):
    base_offset = key_field(key)
    return base_offset.reshape(BATCH_TOKENS, KEY_VALUE_HEADS * HEAD_SIZE).astype(jnp.bfloat16)


def draw_queries(key, part):
    key = jax.random.fold_in(key, 5)
    first_token = jax.random.fold_in(key, 0)
    random_noise = jnp.clip(jax.random.normal(first_token, (BATCH_TOKENS, KEY_VALUE_HEADS, QUERY_HEADS // KEY_VALUE_HEADS, HEAD_SIZE), jnp.float32), -6.0, 6.0)
    return random_noise.reshape(BATCH_TOKENS, QUERY_HEADS * HEAD_SIZE).astype(jnp.bfloat16)


def draw_pair_ids(key, part):
    key = jax.random.fold_in(key, 7)
    order = jax.random.permutation(key, NDOC).astype(jnp.int32)
    halves = order.reshape(NDOC // 2, 2)
    partner = jnp.zeros((NDOC,), jnp.int32)
    partner = partner.at[halves[:, 0]].set(halves[:, 1])
    partner = partner.at[halves[:, 1]].set(halves[:, 0])
    return partner


def block_scale(rng, dims, pieces, smallest, top_value):
    def one(position, parts):
        heights = jax.random.uniform(jax.random.fold_in(jax.random.fold_in(rng, 6), position), (parts,), jnp.float32, smallest / len(pieces), top_value / len(pieces))
        return jnp.repeat(jnp.exp(heights), dims[position] // parts).reshape((-1,) + (1,) * (len(dims) - position - 1))

    factor_of = one(*pieces[0])
    for cut in pieces[1:]:
        factor_of = factor_of * one(*cut)
    return factor_of


def split_up(number_of, total, most, skew):
    weights = [(1 << 20) // math.isqrt(grade ** skew) + 1 for grade in range(2, number_of + 1)]
    rest, counts = total - most - (number_of - 1), [1] * (number_of - 1)
    while rest > 0:
        movable = [i for i in range(number_of - 1) if counts[i] < most]
        whole, left = sum([weights[i] for i in movable]), rest
        for i in movable:
            more = min(most - counts[i], max(1, left * weights[i] // whole), rest)
            counts[i] = counts[i] + more
            rest = rest - more
    return np.array([most] + counts)


def uneven(stream_key, amount, total, reach, skew):
    if amount == 2:
        one = jax.random.randint(stream_key, (), max(1, total - reach), min(reach, total - 1) + 1)
        return jnp.stack([one, total - one])
    sizes = jnp.asarray(split_up(amount, total, reach, skew), jnp.int32)
    couples = (amount - 1) // 2
    source_of, sink = sizes[1:1 + 2 * couples:2], sizes[2:2 + 2 * couples:2]
    margin = jnp.minimum(source_of - 1, reach - sink)
    shifted = jax.random.randint(jax.random.fold_in(stream_key, 1), (couples,), 0, 1 << 20) % (margin + 1)
    sizes = sizes.at[1:1 + 2 * couples:2].set(source_of - shifted).at[2:2 + 2 * couples:2].set(sink + shifted)
    return sizes[jax.random.permutation(jax.random.fold_in(stream_key, 2), amount)]


def scatter_about(stream_key, dims, spread, reach, cuts=(), kind=jnp.bfloat16):
    loudness = block_scale(stream_key, dims, cuts, -0.22, 0.18) if cuts else 1.0
    values = jax.random.normal(stream_key, dims, jnp.float32) * spread * loudness
    return jnp.minimum(jnp.maximum(values, -reach), reach).astype(kind)


def setup_inputs(seed: int = 0) -> dict:
    arg_keys = jax.random.split(jax.random.key(seed), 6)
    queries = draw_queries(jax.random.fold_in(arg_keys[5], 71), 0)
    keys = draw_keys(jax.random.fold_in(arg_keys[5], 71), 0)
    values = scatter_about(arg_keys[2], (BATCH_TOKENS, KEY_VALUE_HEADS * HEAD_SIZE), 1.0, 6.0, ((0, 32),))
    document_lengths = jax.vmap(lambda own: uneven(own, DOCS, WINDOW_TOKENS, LONGEST, 2))(jax.random.split(arg_keys[3], N_DP)).reshape((N_DP, DOCS)).astype(jnp.int32)
    pair_ids = draw_pair_ids(jax.random.fold_in(arg_keys[5], 71), 0)
    return {"queries": queries, "keys": keys, "values": values, "document_lengths": document_lengths, "pair_ids": pair_ids}


SOFTMAX_TEMP = 0.02

def segment_of(lengths, count):
    ends = jnp.cumsum(lengths).astype(jnp.int32)
    places = jnp.arange(count, dtype=jnp.int32)
    return lax.optimization_barrier(jnp.sum((places[:, None] >= ends[None, :]).astype(jnp.int32), axis=1)).astype(jnp.int32)

def attend_head(query_flat, row_segment, key_head, value_head, segment):
    scores = jnp.dot(query_flat, key_head.T, preferred_element_type=jnp.float32) * HEAD_SIZE ** (-0.5)
    scores = jnp.where(row_segment[:, None] == segment[None, :], scores, -jnp.inf)
    largest = lax.optimization_barrier(jnp.max(scores, axis=1, keepdims=True))
    weights = jnp.exp(scores - largest)
    probs = (weights / lax.optimization_barrier(jnp.sum(weights, axis=1, keepdims=True))).astype(jnp.bfloat16)
    return jnp.dot(probs, value_head, preferred_element_type=jnp.float32).astype(jnp.bfloat16)

def pool_row(inputs):
    query_window_row, key_window_row, value_window_row, lengths = inputs
    head_group = QUERY_HEADS // KEY_VALUE_HEADS
    segment = segment_of(lengths, WINDOW_TOKENS)
    row_segment = jnp.repeat(segment, head_group)
    query_head_rows = query_window_row.reshape(WINDOW_TOKENS, KEY_VALUE_HEADS, head_group, HEAD_SIZE)
    key_head_rows = key_window_row.reshape(WINDOW_TOKENS, KEY_VALUE_HEADS, HEAD_SIZE)
    value_head_rows = value_window_row.reshape(WINDOW_TOKENS, KEY_VALUE_HEADS, HEAD_SIZE)
    outputs = []
    for head_number in range(KEY_VALUE_HEADS):
        flat = query_head_rows[:, head_number].reshape(WINDOW_TOKENS * head_group, HEAD_SIZE)
        result = attend_head(flat, row_segment, key_head_rows[:, head_number], value_head_rows[:, head_number], segment)
        outputs.append(result.reshape(WINDOW_TOKENS, head_group, HEAD_SIZE))
    attended = jnp.stack(outputs, axis=1).reshape(WINDOW_TOKENS, QUERY_HEADS * HEAD_SIZE)
    onehot = (segment[None, :] == jnp.arange(DOCS, dtype=jnp.int32)[:, None]).astype(jnp.bfloat16)
    summed = jnp.dot(onehot, attended, preferred_element_type=jnp.float32)
    return summed / lengths[:, None].astype(jnp.float32)

def reference(queries, keys, values, document_lengths, pair_ids):
    packed_rows = (queries.reshape(N_DP, WINDOW_TOKENS, QUERY_HEADS * HEAD_SIZE), keys.reshape(N_DP, WINDOW_TOKENS, KEY_VALUE_HEADS * HEAD_SIZE), values.reshape(N_DP, WINDOW_TOKENS, KEY_VALUE_HEADS * HEAD_SIZE), document_lengths)
    pooled = lax.map(pool_row, packed_rows).reshape(NDOC, QUERY_HEADS * HEAD_SIZE)
    radius = jnp.sqrt(lax.optimization_barrier(jnp.sum(pooled * pooled, axis=1, keepdims=True)) + 1e-06)
    embeddings = (pooled / radius).astype(jnp.bfloat16)
    wide_layout = embeddings.astype(jnp.float32)
    score_logits = jnp.dot(embeddings, embeddings.T, preferred_element_type=jnp.float32) / SOFTMAX_TEMP
    places = jnp.arange(NDOC, dtype=jnp.int32)
    score_logits = jnp.where(places[:, None] == places[None, :], -jnp.inf, score_logits)
    largest = lax.optimization_barrier(jnp.max(score_logits, axis=1, keepdims=True))
    weights = jnp.exp(score_logits - largest)
    probs = weights / lax.optimization_barrier(jnp.sum(weights, axis=1, keepdims=True))
    loss_coefficient = probs - (places[None, :] == pair_ids[:, None]).astype(jnp.float32)
    embedding_gradient = (jnp.dot(loss_coefficient, wide_layout, precision=lax.Precision.HIGHEST) + jnp.dot(loss_coefficient.T, wide_layout, precision=lax.Precision.HIGHEST)) / SOFTMAX_TEMP
    along = lax.optimization_barrier(jnp.sum(wide_layout * embedding_gradient, axis=1, keepdims=True))
    grads = (embedding_gradient - wide_layout * along) / radius
    return (embeddings, grads)
```

```python
import functools
import math

import jax
import jax.numpy as jnp
from jax import lax
from jax.experimental import pallas as pl
from jax.experimental.pallas import tpu as pltpu
from jax.sharding import PartitionSpec as P

QUERY_HEADS = 28
KEY_VALUE_HEADS = 4
HEAD_SIZE = 128
HEAD_GROUP = QUERY_HEADS // KEY_VALUE_HEADS
GROUP_WIDTH = HEAD_GROUP * HEAD_SIZE
PAIR = 2
DOCS = 8
SOFTMAX_TEMP = 0.02
VMEM_LIMIT = 48 * 1024 * 1024

VMEM = pl.BlockSpec(memory_space=pltpu.VMEM)
HBM = pl.BlockSpec(memory_space=pltpu.HBM)


def segments(lengths_ref, places):
    end = lengths_ref[0, 0]
    segment = (places >= end).astype(jnp.int32)
    for d in range(1, DOCS):
        end = end + lengths_ref[0, d]
        segment = segment + (places >= end).astype(jnp.int32)
    return segment


def plan_kernel(parts, lengths_hbm, pairs_hbm, q_hbm, k_hbm, v_hbm, *refs):
    q_out, k_out, v_out, near_out, k_far_out, v_far_out, bias_ref, doc_ref, partner_ref, lengths_ref, pairs_ref, sem, small_sem = refs
    span = k_hbm.shape[0]
    me = lax.axis_index("sp")
    core = lax.rem(me, PAIR)
    small = [
        pltpu.make_async_copy(lengths_hbm, lengths_ref, small_sem.at[0]),
        pltpu.make_async_copy(pairs_hbm, pairs_ref, small_sem.at[1]),
    ]
    for copy in small:
        copy.start()
    copies = []

    def cut(source, other, target, start):
        width = source.shape[1] // KEY_VALUE_HEADS
        for p in range(PAIR):
            first = pl.multiple_of((PAIR * p + (core ^ other)) * width, HEAD_SIZE)
            copies.append(
                pltpu.make_async_copy(
                    source.at[:, pl.ds(first, width)],
                    target.at[:, start + p * width : start + (p + 1) * width],
                    sem.at[len(copies)],
                )
            )

    pair_width = PAIR * HEAD_SIZE
    cut(k_hbm, 0, k_out, 0)
    cut(k_hbm, 1, k_far_out, 0)
    cut(k_hbm, 1, near_out, PAIR * GROUP_WIDTH)
    cut(q_hbm, 1, near_out, 0)
    cut(v_hbm, 1, near_out, PAIR * GROUP_WIDTH + pair_width)
    cut(v_hbm, 0, v_out, 0)
    cut(v_hbm, 1, v_far_out, 0)
    cut(q_hbm, 0, q_out, 0)
    for copy in copies:
        copy.start()
    for copy in small:
        copy.wait()
    doc = lax.broadcasted_iota(jnp.int32, (DOCS, span), 0)
    weight = jnp.zeros((DOCS, span), jnp.float32)
    for d in range(DOCS):
        weight = jnp.where(doc == d, 1.0 / lengths_ref[0, d].astype(jnp.float32), weight)
    row_segments = [
        segments(lengths_ref, (me ^ r) * span + lax.broadcasted_iota(jnp.int32, (span, 1), 0)) for r in range(PAIR)
    ]
    for r in range(parts):
        columns = slice(r * span, (r + 1) * span)
        key_segment = segments(lengths_ref, (me ^ r) * span + lax.broadcasted_iota(jnp.int32, (1, span), 1))
        for t in range(PAIR):
            bias_ref[t * span : (t + 1) * span, columns] = jnp.where(row_segments[t] == key_segment, 0.0, -1e30)
        doc_ref[:, columns] = jnp.where(key_segment == doc, weight, 0.0)
    own = lax.axis_index("dp")
    own_row = lax.broadcasted_iota(jnp.int32, partner_ref.shape, 0)
    own_column = lax.broadcasted_iota(jnp.int32, partner_ref.shape, 1)
    place = jnp.zeros(partner_ref.shape, jnp.int32)
    for d in range(DOCS):
        pair = pairs_ref[d]
        place = jnp.where(own_row == d, ((pair // DOCS) ^ own) * DOCS + lax.rem(pair, DOCS), place)
    partner_ref[...] = jnp.where(own_column == place, 2.0, 0.0)
    for copy in copies:
        copy.wait()


def scores_kernel(bias_ref, q_own, k_own, near, k_far, k_last, sums_ref):
    scale = HEAD_SIZE ** (-0.5) * math.log2(math.e)
    for p in range(PAIR):
        here = slice(p * HEAD_SIZE, (p + 1) * HEAD_SIZE)
        beside = PAIR * GROUP_WIDTH + p * HEAD_SIZE
        key_head = jnp.concatenate(
            [k_own[:, here], near[:, beside : beside + HEAD_SIZE], k_far[:, here], k_last[:, here]], axis=0
        )
        for h in range(HEAD_GROUP):
            place = (p * HEAD_GROUP + h) * HEAD_SIZE
            total = None
            for t, q_ref in enumerate((q_own, near)):
                query = q_ref[:, place : place + HEAD_SIZE]
                rows = query.shape[0]
                scores = lax.dot_general(
                    query, key_head, (((1,), (1,)), ((), ())), preferred_element_type=jnp.float32
                )
                scores = scores + bias_ref[t * rows : (t + 1) * rows]
                largest = jnp.max(scores, axis=1, keepdims=True)
                weights = jnp.exp2((scores - largest) * scale)
                probs = weights * (1.0 / jnp.sum(weights, axis=1, keepdims=True))
                summed = jnp.sum(probs, axis=0, keepdims=True)
                total = summed if total is None else total + summed
            row = p * HEAD_GROUP + h
            sums_ref[row : row + 1] = total


def values_kernel(sums_ref, doc_ref, v_own, near, v_far, v_last, out_ref, sent_ref):
    for p in range(PAIR):
        here = slice(p * HEAD_SIZE, (p + 1) * HEAD_SIZE)
        beside = PAIR * (GROUP_WIDTH + HEAD_SIZE) + p * HEAD_SIZE
        value_head = jnp.concatenate(
            [v_own[:, here], near[:, beside : beside + HEAD_SIZE], v_far[:, here], v_last[:, here]], axis=0
        )
        rows = range(p * HEAD_GROUP, (p + 1) * HEAD_GROUP)
        spread = jnp.concatenate([sums_ref[row : row + 1] * doc_ref[...] for row in rows], axis=0)
        high = spread.astype(jnp.bfloat16)
        low = (spread - high.astype(jnp.float32)).astype(jnp.bfloat16)
        summed = jnp.dot(high, value_head, preferred_element_type=jnp.float32) + jnp.dot(
            low, value_head, preferred_element_type=jnp.float32
        )
        for h, row in enumerate(rows):
            out_ref[:, row * HEAD_SIZE : (row + 1) * HEAD_SIZE] = summed[h * DOCS : (h + 1) * DOCS]
    sent_ref[...] = out_ref[...].astype(jnp.bfloat16)


def pool_kernel(one_ref, two_ref, pooled_ref, sent_ref):
    pooled = one_ref[...] + two_ref[...].astype(jnp.float32)
    pooled_ref[...] = pooled
    sent_ref[...] = pooled.astype(jnp.bfloat16)


def join_kernel(*refs):
    refs[-1][...] = jnp.concatenate([ref[...] for ref in in_order(refs[:-1])], axis=0)


def in_order(refs):
    return (refs[0], *refs[:0:-1])


def gram_kernel(*refs):
    every = jnp.concatenate([ref[...] for ref in in_order(refs[:-1])], axis=0)
    refs[-1][...] = lax.dot_general(every, every, (((1,), (1,)), ((), ())), preferred_element_type=jnp.float32)


def grads_kernel(partner_ref, pooled_ref, gram_one, gram_two, *refs):
    every_refs, (emb_ref, grads_ref) = refs[:-2], refs[-2:]
    gram = gram_one[...] + gram_two[...]
    docs = gram.shape[0]
    columns = pl.ds(pl.multiple_of((lax.axis_index("sp") // PAIR) * GROUP_WIDTH, HEAD_SIZE), GROUP_WIDTH)
    row = lax.broadcasted_iota(jnp.int32, (docs, docs), 0)
    column = lax.broadcasted_iota(jnp.int32, (docs, docs), 1)
    diagonal = row == column
    square = jnp.where(diagonal, gram, 0.0)
    inverse_column = lax.rsqrt(jnp.sum(square, axis=1, keepdims=True) + 1e-6)
    inverse_row = lax.rsqrt(jnp.sum(square, axis=0, keepdims=True) + 1e-6)
    cosine = gram * inverse_column * inverse_row
    logits = jnp.where(diagonal, -jnp.inf, cosine * (1.0 / SOFTMAX_TEMP))
    own = logits[:DOCS]
    largest = jnp.max(own, axis=1, keepdims=True)
    weights = jnp.exp(own - largest)
    probs = weights / jnp.sum(weights, axis=1, keepdims=True)
    largest_row = jnp.max(logits, axis=0, keepdims=True)
    total_row = jnp.sum(jnp.exp(logits - largest_row), axis=0, keepdims=True)
    probs = probs + jnp.exp(own - largest_row) / total_row
    both = probs - partner_ref[...]
    along = jnp.sum(both * cosine[:DOCS], axis=1, keepdims=True) * (1.0 / SOFTMAX_TEMP)
    weighted = both * inverse_row * (1.0 / SOFTMAX_TEMP)
    high = weighted.astype(jnp.bfloat16)
    low = (weighted - high.astype(jnp.float32)).astype(jnp.bfloat16)
    every = jnp.concatenate([ref[:, columns] for ref in in_order(every_refs)], axis=0)
    gradient = jnp.dot(high, every, preferred_element_type=jnp.float32) + jnp.dot(
        low, every, preferred_element_type=jnp.float32
    )
    inverse = inverse_column[:DOCS]
    embeddings = (pooled_ref[:, columns] * inverse).astype(jnp.bfloat16)
    emb_ref[...] = embeddings
    grads_ref[...] = (gradient - embeddings.astype(jnp.float32) * along) * inverse


def call(kernel, out_shape, in_specs, scratch_shapes=(), flops=0, moved=0):
    return pl.pallas_call(
        kernel,
        out_shape=out_shape,
        in_specs=in_specs,
        out_specs=jax.tree.map(lambda _: VMEM, out_shape),
        scratch_shapes=scratch_shapes,
        compiler_params=pltpu.CompilerParams(vmem_limit_bytes=VMEM_LIMIT),
        cost_estimate=pl.CostEstimate(flops=flops, bytes_accessed=moved, transcendentals=0),
    )


def swap(block, axis, size, distance):
    return lax.ppermute(block, axis, [(s, s ^ distance) for s in range(size)])


def gather_pairs(block, axis, size):
    have, blocks = 1, [block]
    while have < size:
        if have > 1:
            shape = (len(blocks) * block.shape[0], block.shape[1])
            block = call(join_kernel, jax.ShapeDtypeStruct(shape, block.dtype), [VMEM] * len(blocks))(*blocks)
        radix = PAIR if have == 1 else min(4, size // have)
        blocks = [block] + [swap(block, axis, size, r * have) for r in reversed(range(1, radix))]
        have *= radix
    return blocks


def per_device(sizes, queries, keys, values, document_lengths, pair_ids):
    replicas, parts = sizes
    tokens, features = queries.shape
    width = features // PAIR
    kv_width = keys.shape[1] // PAIR
    docs = DOCS * replicas
    f32, bf16 = jnp.float32, jnp.bfloat16
    struct = jax.ShapeDtypeStruct
    query_own, key_own, value_own, near, key_send, value_send, bias, of_doc, partner = call(
        functools.partial(plan_kernel, parts),
        (
            struct((tokens, width), bf16),
            struct((tokens, kv_width), bf16),
            struct((tokens, kv_width), bf16),
            struct((tokens, width + 2 * kv_width), bf16),
            struct((tokens, kv_width), bf16),
            struct((tokens, kv_width), bf16),
            struct((PAIR * tokens, parts * tokens), f32),
            struct((DOCS, parts * tokens), f32),
            struct((DOCS, docs), f32),
        ),
        [HBM] * 5,
        [
            pltpu.SMEM((1, DOCS), jnp.int32),
            pltpu.SMEM((DOCS,), jnp.int32),
            pltpu.SemaphoreType.DMA((8 * PAIR,)),
            pltpu.SemaphoreType.DMA((2,)),
        ],
        moved=2 * tokens * features + 4 * keys.size,
    )(*(pltpu.with_memory_space_constraint(x, pltpu.HBM) for x in (document_lengths, pair_ids, queries, keys, values)))
    near = swap(near, "sp", parts, 1)
    value_far = swap(value_own, "sp", parts, 2)
    value_last = swap(value_send, "sp", parts, 3)
    key_far = swap(key_own, "sp", parts, 2)
    key_last = swap(key_send, "sp", parts, 3)
    sums = call(
        scores_kernel,
        struct((PAIR * HEAD_GROUP, parts * tokens), f32),
        [VMEM] * 6,
        flops=tokens * features * tokens * parts,
        moved=2 * queries.size + 4 * parts * keys.size,
    )(bias, query_own, key_own, near, key_far, key_last)
    partial, rounded = call(
        values_kernel, (struct((DOCS, width), f32), struct((DOCS, width), bf16)), [VMEM] * 6
    )(sums, of_doc, value_own, near, value_far, value_last)
    pooled, sent = call(
        pool_kernel, (struct((DOCS, width), f32), struct((DOCS, width), bf16)), [VMEM] * 2
    )(partial, swap(rounded, "sp", parts, 2))
    blocks = gather_pairs(sent, "dp", replicas)
    gram = call(gram_kernel, struct((docs, docs), f32), [VMEM] * len(blocks))(*blocks)
    return call(
        grads_kernel,
        (struct((DOCS, features // parts), bf16), struct((DOCS, features // parts), f32)),
        [VMEM] * (4 + len(blocks)),
    )(partner, pooled, gram, swap(gram, "sp", parts, 1), *blocks)


def solution(mesh):
    sizes = (mesh.shape["dp"], mesh.shape["sp"])
    return jax.shard_map(
        functools.partial(per_device, sizes),
        mesh=mesh,
        in_specs=(
            P(("dp", "sp"), None),
            P(("dp", "sp"), None),
            P(("dp", "sp"), None),
            P("dp", None),
            P("dp"),
        ),
        out_specs=(P("dp", "sp"), P("dp", "sp")),
        check_vma=False,
    )
```

```python
import functools
import math

import jax
import jax.numpy as jnp
from jax import lax
from jax.experimental import pallas as pl
from jax.experimental.pallas import tpu as pltpu
from jax.sharding import PartitionSpec as P

QUERY_HEADS = 28
KEY_VALUE_HEADS = 4
HEAD_SIZE = 128
HEAD_GROUP = QUERY_HEADS // KEY_VALUE_HEADS
GROUP_WIDTH = HEAD_GROUP * HEAD_SIZE
PAIR = 2
DOCS = 8
SOFTMAX_TEMP = 0.02
VMEM_LIMIT = 48 * 1024 * 1024

VMEM = pl.BlockSpec(memory_space=pltpu.VMEM)
HBM = pl.BlockSpec(memory_space=pltpu.HBM)


def segments(lengths_ref, places):
    end = lengths_ref[0, 0]
    segment = (places >= end).astype(jnp.int32)
    for d in range(1, DOCS):
        end = end + lengths_ref[0, d]
        segment = segment + (places >= end).astype(jnp.int32)
    return segment


def group_of(p, role):
    return role if p == 0 else KEY_VALUE_HEADS - 1 - role


def plan_kernel(parts, lengths_hbm, pairs_hbm, q_hbm, k_hbm, v_hbm, *refs):
    q_out, k_out, v_out, near_out, k_far_out, v_far_out, bias_ref, doc_ref, partner_ref, lengths_ref, pairs_ref, sem, small_sem = refs
    span = k_hbm.shape[0]
    me = lax.axis_index("sp")
    role = lax.rem(me, PAIR) ^ (me // PAIR)
    small = [
        pltpu.make_async_copy(lengths_hbm, lengths_ref, small_sem.at[0]),
        pltpu.make_async_copy(pairs_hbm, pairs_ref, small_sem.at[1]),
    ]
    for copy in small:
        copy.start()
    copies = []

    def cut(source, other, target, start):
        width = source.shape[1] // KEY_VALUE_HEADS
        for p in range(PAIR):
            first = pl.multiple_of(group_of(p, role ^ other) * width, HEAD_SIZE)
            copies.append(
                pltpu.make_async_copy(
                    source.at[:, pl.ds(first, width)],
                    target.at[:, start + p * width : start + (p + 1) * width],
                    sem.at[len(copies)],
                )
            )

    pair_width = PAIR * HEAD_SIZE
    cut(k_hbm, 0, k_out, 0)
    cut(k_hbm, 1, k_far_out, 0)
    cut(k_hbm, 1, near_out, PAIR * GROUP_WIDTH)
    cut(q_hbm, 1, near_out, 0)
    cut(v_hbm, 1, near_out, PAIR * GROUP_WIDTH + pair_width)
    cut(v_hbm, 0, v_out, 0)
    cut(v_hbm, 1, v_far_out, 0)
    cut(q_hbm, 0, q_out, 0)
    for copy in copies:
        copy.start()
    for copy in small:
        copy.wait()
    doc = lax.broadcasted_iota(jnp.int32, (DOCS, span), 0)
    weight = jnp.zeros((DOCS, span), jnp.float32)
    for d in range(DOCS):
        weight = jnp.where(doc == d, 1.0 / lengths_ref[0, d].astype(jnp.float32), weight)
    row_segments = [
        segments(lengths_ref, (me ^ r) * span + lax.broadcasted_iota(jnp.int32, (span, 1), 0)) for r in range(PAIR)
    ]
    for r in range(parts):
        columns = slice(r * span, (r + 1) * span)
        key_segment = segments(lengths_ref, (me ^ r) * span + lax.broadcasted_iota(jnp.int32, (1, span), 1))
        for t in range(PAIR):
            bias_ref[t * span : (t + 1) * span, columns] = jnp.where(row_segments[t] == key_segment, 0.0, -1e30)
        doc_ref[:, columns] = jnp.where(key_segment == doc, weight, 0.0)
    own = lax.axis_index("dp")
    own_row = lax.broadcasted_iota(jnp.int32, partner_ref.shape, 0)
    own_column = lax.broadcasted_iota(jnp.int32, partner_ref.shape, 1)
    place = jnp.zeros(partner_ref.shape, jnp.int32)
    for d in range(DOCS):
        pair = pairs_ref[d]
        place = jnp.where(own_row == d, ((pair // DOCS) ^ own) * DOCS + lax.rem(pair, DOCS), place)
    partner_ref[...] = jnp.where(own_column == place, 2.0, 0.0)
    for copy in copies:
        copy.wait()


def scores_kernel(bias_ref, q_own, k_own, near, k_far, k_last, sums_ref):
    scale = HEAD_SIZE ** (-0.5) * math.log2(math.e)
    for p in range(PAIR):
        here = slice(p * HEAD_SIZE, (p + 1) * HEAD_SIZE)
        beside = PAIR * GROUP_WIDTH + p * HEAD_SIZE
        key_head = jnp.concatenate(
            [k_own[:, here], near[:, beside : beside + HEAD_SIZE], k_far[:, here], k_last[:, here]], axis=0
        )
        for h in range(HEAD_GROUP):
            place = (p * HEAD_GROUP + h) * HEAD_SIZE
            total = None
            for t, q_ref in enumerate((q_own, near)):
                query = q_ref[:, place : place + HEAD_SIZE]
                rows = query.shape[0]
                scores = lax.dot_general(
                    query, key_head, (((1,), (1,)), ((), ())), preferred_element_type=jnp.float32
                )
                scores = scores + bias_ref[t * rows : (t + 1) * rows]
                largest = jnp.max(scores, axis=1, keepdims=True)
                weights = jnp.exp2((scores - largest) * scale)
                probs = weights * (1.0 / jnp.sum(weights, axis=1, keepdims=True))
                summed = jnp.sum(probs, axis=0, keepdims=True)
                total = summed if total is None else total + summed
            row = p * HEAD_GROUP + h
            sums_ref[row : row + 1] = total


def values_kernel(sums_ref, doc_ref, v_own, near, v_far, v_last, out_ref, sent_ref):
    for p in range(PAIR):
        here = slice(p * HEAD_SIZE, (p + 1) * HEAD_SIZE)
        beside = PAIR * (GROUP_WIDTH + HEAD_SIZE) + p * HEAD_SIZE
        value_head = jnp.concatenate(
            [v_own[:, here], near[:, beside : beside + HEAD_SIZE], v_far[:, here], v_last[:, here]], axis=0
        )
        rows = range(p * HEAD_GROUP, (p + 1) * HEAD_GROUP)
        spread = jnp.concatenate([sums_ref[row : row + 1] * doc_ref[...] for row in rows], axis=0)
        high = spread.astype(jnp.bfloat16)
        low = (spread - high.astype(jnp.float32)).astype(jnp.bfloat16)
        summed = jnp.dot(high, value_head, preferred_element_type=jnp.float32) + jnp.dot(
            low, value_head, preferred_element_type=jnp.float32
        )
        for h, row in enumerate(rows):
            out_ref[:, row * HEAD_SIZE : (row + 1) * HEAD_SIZE] = summed[h * DOCS : (h + 1) * DOCS]
    sent_ref[...] = out_ref[...].astype(jnp.bfloat16)


def pool_kernel(one_ref, two_ref, pooled_ref, sent_ref):
    pooled = one_ref[...] + two_ref[...].astype(jnp.float32)
    pooled_ref[...] = pooled
    sent_ref[...] = pooled.astype(jnp.bfloat16)


def join_kernel(*refs):
    refs[-1][...] = jnp.concatenate([ref[...] for ref in in_order(refs[:-1])], axis=0)


def in_order(refs):
    return (refs[0], *refs[:0:-1])


def gram_kernel(*refs):
    every = jnp.concatenate([ref[...] for ref in in_order(refs[:-1])], axis=0)
    refs[-1][...] = lax.dot_general(every, every, (((1,), (1,)), ((), ())), preferred_element_type=jnp.float32)


def grads_kernel(partner_ref, pooled_ref, gram_one, gram_two, *refs):
    every_refs, (emb_ref, grads_ref) = refs[:-2], refs[-2:]
    gram = gram_one[...] + gram_two[...]
    docs = gram.shape[0]
    columns = pl.ds(pl.multiple_of((lax.axis_index("sp") // PAIR) * GROUP_WIDTH, HEAD_SIZE), GROUP_WIDTH)
    row = lax.broadcasted_iota(jnp.int32, (docs, docs), 0)
    column = lax.broadcasted_iota(jnp.int32, (docs, docs), 1)
    diagonal = row == column
    square = jnp.where(diagonal, gram, 0.0)
    inverse_column = lax.rsqrt(jnp.sum(square, axis=1, keepdims=True) + 1e-6)
    inverse_row = lax.rsqrt(jnp.sum(square, axis=0, keepdims=True) + 1e-6)
    cosine = gram * inverse_column * inverse_row
    logits = jnp.where(diagonal, -jnp.inf, cosine * (1.0 / SOFTMAX_TEMP))
    own = logits[:DOCS]
    largest = jnp.max(own, axis=1, keepdims=True)
    weights = jnp.exp(own - largest)
    probs = weights / jnp.sum(weights, axis=1, keepdims=True)
    largest_row = jnp.max(logits, axis=0, keepdims=True)
    total_row = jnp.sum(jnp.exp(logits - largest_row), axis=0, keepdims=True)
    probs = probs + jnp.exp(own - largest_row) / total_row
    both = probs - partner_ref[...]
    along = jnp.sum(both * cosine[:DOCS], axis=1, keepdims=True) * (1.0 / SOFTMAX_TEMP)
    weighted = both * inverse_row * (1.0 / SOFTMAX_TEMP)
    high = weighted.astype(jnp.bfloat16)
    low = (weighted - high.astype(jnp.float32)).astype(jnp.bfloat16)
    every = jnp.concatenate([ref[:, columns] for ref in in_order(every_refs)], axis=0)
    gradient = jnp.dot(high, every, preferred_element_type=jnp.float32) + jnp.dot(
        low, every, preferred_element_type=jnp.float32
    )
    inverse = inverse_column[:DOCS]
    embeddings = (pooled_ref[:, columns] * inverse).astype(jnp.bfloat16)
    emb_ref[...] = embeddings
    grads_ref[...] = (gradient - embeddings.astype(jnp.float32) * along) * inverse


def call(kernel, out_shape, in_specs, scratch_shapes=(), flops=0, moved=0):
    return pl.pallas_call(
        kernel,
        out_shape=out_shape,
        in_specs=in_specs,
        out_specs=jax.tree.map(lambda _: VMEM, out_shape),
        scratch_shapes=scratch_shapes,
        compiler_params=pltpu.CompilerParams(vmem_limit_bytes=VMEM_LIMIT),
        cost_estimate=pl.CostEstimate(flops=flops, bytes_accessed=moved, transcendentals=0),
    )


def swap(block, axis, size, distance):
    return lax.ppermute(block, axis, [(s, s ^ distance) for s in range(size)])


def gather_pairs(block, axis, size):
    have, blocks = 1, [block]
    while have < size:
        if have > 1:
            shape = (len(blocks) * block.shape[0], block.shape[1])
            block = call(join_kernel, jax.ShapeDtypeStruct(shape, block.dtype), [VMEM] * len(blocks))(*blocks)
        radix = PAIR if have == 1 else min(4, size // have)
        blocks = [block] + [swap(block, axis, size, r * have) for r in reversed(range(1, radix))]
        have *= radix
    return blocks


def per_device(sizes, queries, keys, values, document_lengths, pair_ids):
    replicas, parts = sizes
    tokens, features = queries.shape
    width = features // PAIR
    kv_width = keys.shape[1] // PAIR
    docs = DOCS * replicas
    f32, bf16 = jnp.float32, jnp.bfloat16
    struct = jax.ShapeDtypeStruct
    query_own, key_own, value_own, near, key_send, value_send, bias, of_doc, partner = call(
        functools.partial(plan_kernel, parts),
        (
            struct((tokens, width), bf16),
            struct((tokens, kv_width), bf16),
            struct((tokens, kv_width), bf16),
            struct((tokens, width + 2 * kv_width), bf16),
            struct((tokens, kv_width), bf16),
            struct((tokens, kv_width), bf16),
            struct((PAIR * tokens, parts * tokens), f32),
            struct((DOCS, parts * tokens), f32),
            struct((DOCS, docs), f32),
        ),
        [HBM] * 5,
        [
            pltpu.SMEM((1, DOCS), jnp.int32),
            pltpu.SMEM((DOCS,), jnp.int32),
            pltpu.SemaphoreType.DMA((8 * PAIR,)),
            pltpu.SemaphoreType.DMA((2,)),
        ],
        moved=2 * tokens * features + 4 * keys.size,
    )(*(pltpu.with_memory_space_constraint(x, pltpu.HBM) for x in (document_lengths, pair_ids, queries, keys, values)))
    near = swap(near, "sp", parts, 1)
    value_far = swap(value_send, "sp", parts, 2)
    value_last = swap(value_own, "sp", parts, 3)
    key_far = swap(key_send, "sp", parts, 2)
    key_last = swap(key_own, "sp", parts, 3)
    sums = call(
        scores_kernel,
        struct((PAIR * HEAD_GROUP, parts * tokens), f32),
        [VMEM] * 6,
        flops=tokens * features * tokens * parts,
        moved=2 * queries.size + 4 * parts * keys.size,
    )(bias, query_own, key_own, near, key_far, key_last)
    partial, rounded = call(
        values_kernel, (struct((DOCS, width), f32), struct((DOCS, width), bf16)), [VMEM] * 6
    )(sums, of_doc, value_own, near, value_far, value_last)
    pooled, sent = call(
        pool_kernel, (struct((DOCS, width), f32), struct((DOCS, width), bf16)), [VMEM] * 2
    )(partial, swap(rounded, "sp", parts, 3))
    blocks = gather_pairs(sent, "dp", replicas)
    gram = call(gram_kernel, struct((docs, docs), f32), [VMEM] * len(blocks))(*blocks)
    return call(
        grads_kernel,
        (struct((DOCS, features // parts), bf16), struct((DOCS, features // parts), f32)),
        [VMEM] * (4 + len(blocks)),
    )(partner, pooled, gram, swap(gram, "sp", parts, 1), *blocks)


def solution(mesh):
    sizes = (mesh.shape["dp"], mesh.shape["sp"])
    return jax.shard_map(
        functools.partial(per_device, sizes),
        mesh=mesh,
        in_specs=(
            P(("dp", "sp"), None),
            P(("dp", "sp"), None),
            P(("dp", "sp"), None),
            P("dp", None),
            P("dp"),
        ),
        out_specs=(P("dp", "sp"), P("dp", "sp")),
        check_vma=False,
    )
```

```python
import functools
import math

import jax
import jax.numpy as jnp
from jax import lax
from jax.experimental import pallas as pl
from jax.experimental.pallas import tpu as pltpu
from jax.sharding import PartitionSpec as P

QUERY_HEADS = 28
KEY_VALUE_HEADS = 4
HEAD_SIZE = 128
HEAD_GROUP = QUERY_HEADS // KEY_VALUE_HEADS
GROUP_WIDTH = HEAD_GROUP * HEAD_SIZE
PAIR = 2
DOCS = 8
SOFTMAX_TEMP = 0.02
VMEM_LIMIT = 48 * 1024 * 1024

VMEM = pl.BlockSpec(memory_space=pltpu.VMEM)
HBM = pl.BlockSpec(memory_space=pltpu.HBM)


def segments(lengths_ref, places):
    end = lengths_ref[0, 0]
    segment = (places >= end).astype(jnp.int32)
    for d in range(1, DOCS):
        end = end + lengths_ref[0, d]
        segment = segment + (places >= end).astype(jnp.int32)
    return segment


def plan_kernel(parts, lengths_hbm, pairs_hbm, q_hbm, k_hbm, v_hbm, *refs):
    q_out, k_out, v_out, near_out, k_far_out, v_far_out, bias_ref, doc_ref, partner_ref, lengths_ref, pairs_ref, sem, small_sem = refs
    span = k_hbm.shape[0]
    me = lax.axis_index("sp")
    core = lax.rem(me, PAIR)
    small = [
        pltpu.make_async_copy(lengths_hbm, lengths_ref, small_sem.at[0]),
        pltpu.make_async_copy(pairs_hbm, pairs_ref, small_sem.at[1]),
    ]
    for copy in small:
        copy.start()
    copies = []

    def cut(source, other, target, start):
        width = source.shape[1] // KEY_VALUE_HEADS
        for p in range(PAIR):
            first = pl.multiple_of((PAIR * p + (core ^ other)) * width, HEAD_SIZE)
            copies.append(
                pltpu.make_async_copy(
                    source.at[:, pl.ds(first, width)],
                    target.at[:, start + p * width : start + (p + 1) * width],
                    sem.at[len(copies)],
                )
            )

    pair_width = PAIR * HEAD_SIZE
    cut(k_hbm, 0, k_out, 0)
    cut(k_hbm, 1, k_far_out, 0)
    cut(k_hbm, 1, near_out, PAIR * GROUP_WIDTH)
    cut(q_hbm, 1, near_out, 0)
    cut(v_hbm, 1, near_out, PAIR * GROUP_WIDTH + pair_width)
    cut(v_hbm, 0, v_out, 0)
    cut(v_hbm, 1, v_far_out, 0)
    cut(q_hbm, 0, q_out, 0)
    for copy in copies:
        copy.start()
    for copy in small:
        copy.wait()
    doc = lax.broadcasted_iota(jnp.int32, (DOCS, span), 0)
    weight = jnp.zeros((DOCS, span), jnp.float32)
    for d in range(DOCS):
        weight = jnp.where(doc == d, 1.0 / lengths_ref[0, d].astype(jnp.float32), weight)
    row_segments = [
        segments(lengths_ref, (me ^ r) * span + lax.broadcasted_iota(jnp.int32, (span, 1), 0)) for r in range(PAIR)
    ]
    for r in range(parts):
        columns = slice(r * span, (r + 1) * span)
        key_segment = segments(lengths_ref, (me ^ r) * span + lax.broadcasted_iota(jnp.int32, (1, span), 1))
        for t in range(PAIR):
            bias_ref[t * span : (t + 1) * span, columns] = jnp.where(row_segments[t] == key_segment, 0.0, -1e30)
        doc_ref[:, columns] = jnp.where(key_segment == doc, weight, 0.0)
    own = lax.axis_index("dp")
    own_row = lax.broadcasted_iota(jnp.int32, partner_ref.shape, 0)
    own_column = lax.broadcasted_iota(jnp.int32, partner_ref.shape, 1)
    place = jnp.zeros(partner_ref.shape, jnp.int32)
    for d in range(DOCS):
        pair = pairs_ref[d]
        place = jnp.where(own_row == d, ((pair // DOCS) ^ own) * DOCS + lax.rem(pair, DOCS), place)
    partner_ref[...] = jnp.where(own_column == place, 2.0, 0.0)
    for copy in copies:
        copy.wait()


def scores_kernel(bias_ref, q_own, k_own, near, k_far, k_last, sums_ref):
    scale = HEAD_SIZE ** (-0.5) * math.log2(math.e)
    for p in range(PAIR):
        here = slice(p * HEAD_SIZE, (p + 1) * HEAD_SIZE)
        beside = PAIR * GROUP_WIDTH + p * HEAD_SIZE
        key_head = jnp.concatenate(
            [k_own[:, here], near[:, beside : beside + HEAD_SIZE], k_far[:, here], k_last[:, here]], axis=0
        )
        for h in range(HEAD_GROUP):
            place = (p * HEAD_GROUP + h) * HEAD_SIZE
            total = None
            for t, q_ref in enumerate((q_own, near)):
                query = q_ref[:, place : place + HEAD_SIZE]
                rows = query.shape[0]
                scores = lax.dot_general(
                    query, key_head, (((1,), (1,)), ((), ())), preferred_element_type=jnp.float32
                )
                scores = scores + bias_ref[t * rows : (t + 1) * rows]
                largest = jnp.max(scores, axis=1, keepdims=True)
                weights = jnp.exp2((scores - largest) * scale)
                probs = weights * (1.0 / jnp.sum(weights, axis=1, keepdims=True))
                summed = jnp.sum(probs, axis=0, keepdims=True)
                total = summed if total is None else total + summed
            row = p * HEAD_GROUP + h
            sums_ref[row : row + 1] = total


def values_kernel(sums_ref, doc_ref, v_own, near, v_far, v_last, out_ref, sent_ref):
    for p in range(PAIR):
        here = slice(p * HEAD_SIZE, (p + 1) * HEAD_SIZE)
        beside = PAIR * (GROUP_WIDTH + HEAD_SIZE) + p * HEAD_SIZE
        value_head = jnp.concatenate(
            [v_own[:, here], near[:, beside : beside + HEAD_SIZE], v_far[:, here], v_last[:, here]], axis=0
        )
        rows = range(p * HEAD_GROUP, (p + 1) * HEAD_GROUP)
        spread = jnp.concatenate([sums_ref[row : row + 1] * doc_ref[...] for row in rows], axis=0)
        high = spread.astype(jnp.bfloat16)
        low = (spread - high.astype(jnp.float32)).astype(jnp.bfloat16)
        summed = jnp.dot(high, value_head, preferred_element_type=jnp.float32) + jnp.dot(
            low, value_head, preferred_element_type=jnp.float32
        )
        for h, row in enumerate(rows):
            out_ref[:, row * HEAD_SIZE : (row + 1) * HEAD_SIZE] = summed[h * DOCS : (h + 1) * DOCS]
    sent_ref[...] = out_ref[...].astype(jnp.bfloat16)


def pool_kernel(corner_ref, far_ref, next_ref, own_ref, sent_ref):
    pooled = own_ref[...] + far_ref[...].astype(jnp.float32)
    beside = next_ref[...].astype(jnp.float32) + corner_ref[...].astype(jnp.float32)
    sent_ref[...] = jnp.concatenate([pooled, beside], axis=0).astype(jnp.bfloat16)


def in_order(refs):
    return (refs[-1], *refs[-3::-1], refs[-2])


def join_kernel(*refs):
    refs[-1][...] = jnp.concatenate([ref[...] for ref in in_order(refs[:-1])], axis=0)


def gram_kernel(*refs):
    every = jnp.concatenate([ref[...] for ref in in_order(refs[:-1])], axis=0)
    refs[-1][...] = lax.dot_general(every, every, (((1,), (1,)), ((), ())), preferred_element_type=jnp.float32)


def grads_kernel(partner_ref, gram_one, gram_two, *refs):
    every_refs, (own_ref, far_ref, emb_ref, grads_ref) = refs[:-4], refs[-4:]
    gram = gram_one[...] + gram_two[...]
    docs = gram.shape[0]
    columns = pl.ds(pl.multiple_of((lax.axis_index("sp") // PAIR) * GROUP_WIDTH, HEAD_SIZE), GROUP_WIDTH)
    row = lax.broadcasted_iota(jnp.int32, (docs, docs), 0)
    column = lax.broadcasted_iota(jnp.int32, (docs, docs), 1)
    diagonal = row == column
    square = jnp.where(diagonal, gram, 0.0)
    inverse_column = lax.rsqrt(jnp.sum(square, axis=1, keepdims=True) + 1e-6)
    inverse_row = lax.rsqrt(jnp.sum(square, axis=0, keepdims=True) + 1e-6)
    cosine = gram * inverse_column * inverse_row
    logits = jnp.where(diagonal, -jnp.inf, cosine * (1.0 / SOFTMAX_TEMP))
    own = logits[:DOCS]
    largest = jnp.max(own, axis=1, keepdims=True)
    weights = jnp.exp(own - largest)
    probs = weights / jnp.sum(weights, axis=1, keepdims=True)
    largest_row = jnp.max(logits, axis=0, keepdims=True)
    total_row = jnp.sum(jnp.exp(logits - largest_row), axis=0, keepdims=True)
    probs = probs + jnp.exp(own - largest_row) / total_row
    both = probs - partner_ref[...]
    along = jnp.sum(both * cosine[:DOCS], axis=1, keepdims=True) * (1.0 / SOFTMAX_TEMP)
    weighted = both * inverse_row * (1.0 / SOFTMAX_TEMP)
    high = weighted.astype(jnp.bfloat16)
    low = (weighted - high.astype(jnp.float32)).astype(jnp.bfloat16)
    every = jnp.concatenate([ref[:, columns] for ref in in_order(every_refs)], axis=0)
    gradient = jnp.dot(high, every, preferred_element_type=jnp.float32) + jnp.dot(
        low, every, preferred_element_type=jnp.float32
    )
    inverse = inverse_column[:DOCS]
    pooled = own_ref[:, columns] + far_ref[:, columns].astype(jnp.float32)
    embeddings = (pooled * inverse).astype(jnp.bfloat16)
    emb_ref[...] = embeddings
    grads_ref[...] = (gradient - embeddings.astype(jnp.float32) * along) * inverse


def call(kernel, out_shape, in_specs, scratch_shapes=(), flops=0, moved=0):
    return pl.pallas_call(
        kernel,
        out_shape=out_shape,
        in_specs=in_specs,
        out_specs=jax.tree.map(lambda _: VMEM, out_shape),
        scratch_shapes=scratch_shapes,
        compiler_params=pltpu.CompilerParams(vmem_limit_bytes=VMEM_LIMIT),
        cost_estimate=pl.CostEstimate(flops=flops, bytes_accessed=moved, transcendentals=0),
    )


def swap(block, axis, size, distance):
    return lax.ppermute(block, axis, [(s, s ^ distance) for s in range(size)])


def gather_pairs(block, axis, size):
    have, blocks = PAIR, [block]
    while have < size:
        if have > PAIR:
            shape = (len(blocks) * block.shape[0], block.shape[1])
            block = call(join_kernel, jax.ShapeDtypeStruct(shape, block.dtype), [VMEM] * len(blocks))(*blocks)
        radix = min(4, size // have)
        blocks = [swap(block, axis, size, r * have) for r in (*range(radix - 2, 0, -1), radix - 1)] + [block]
        have *= radix
    return blocks


def per_device(sizes, queries, keys, values, document_lengths, pair_ids):
    replicas, parts = sizes
    tokens, features = queries.shape
    width = features // PAIR
    kv_width = keys.shape[1] // PAIR
    docs = DOCS * replicas
    f32, bf16 = jnp.float32, jnp.bfloat16
    struct = jax.ShapeDtypeStruct
    query_own, key_own, value_own, near, key_send, value_send, bias, of_doc, partner = call(
        functools.partial(plan_kernel, parts),
        (
            struct((tokens, width), bf16),
            struct((tokens, kv_width), bf16),
            struct((tokens, kv_width), bf16),
            struct((tokens, width + 2 * kv_width), bf16),
            struct((tokens, kv_width), bf16),
            struct((tokens, kv_width), bf16),
            struct((PAIR * tokens, parts * tokens), f32),
            struct((DOCS, parts * tokens), f32),
            struct((DOCS, docs), f32),
        ),
        [HBM] * 5,
        [
            pltpu.SMEM((1, DOCS), jnp.int32),
            pltpu.SMEM((DOCS,), jnp.int32),
            pltpu.SemaphoreType.DMA((8 * PAIR,)),
            pltpu.SemaphoreType.DMA((2,)),
        ],
        moved=2 * tokens * features + 4 * keys.size,
    )(*(pltpu.with_memory_space_constraint(x, pltpu.HBM) for x in (document_lengths, pair_ids, queries, keys, values)))
    near = swap(near, "sp", parts, 1)
    value_far = swap(value_own, "sp", parts, 2)
    value_last = swap(value_send, "sp", parts, 3)
    key_far = swap(key_own, "sp", parts, 2)
    key_last = swap(key_send, "sp", parts, 3)
    sums = call(
        scores_kernel,
        struct((PAIR * HEAD_GROUP, parts * tokens), f32),
        [VMEM] * 6,
        flops=tokens * features * tokens * parts,
        moved=2 * queries.size + 4 * parts * keys.size,
    )(bias, query_own, key_own, near, key_far, key_last)
    partial, rounded = call(
        values_kernel, (struct((DOCS, width), f32), struct((DOCS, width), bf16)), [VMEM] * 6
    )(sums, of_doc, value_own, near, value_far, value_last)
    corner = swap(rounded, ("dp", "sp"), replicas * parts, parts + 2)
    far = swap(rounded, "sp", parts, 2)
    beside = swap(rounded, "dp", replicas, 1)
    sent = call(pool_kernel, struct((PAIR * DOCS, width), bf16), [VMEM] * 4)(corner, far, beside, partial)
    blocks = gather_pairs(sent, "dp", replicas)
    gram = call(gram_kernel, struct((docs, docs), f32), [VMEM] * len(blocks))(*blocks)
    return call(
        grads_kernel,
        (struct((DOCS, features // parts), bf16), struct((DOCS, features // parts), f32)),
        [VMEM] * (5 + len(blocks)),
    )(partner, gram, swap(gram, "sp", parts, 1), *blocks, partial, far)


def solution(mesh):
    sizes = (mesh.shape["dp"], mesh.shape["sp"])
    return jax.shard_map(
        functools.partial(per_device, sizes),
        mesh=mesh,
        in_specs=(
            P(("dp", "sp"), None),
            P(("dp", "sp"), None),
            P(("dp", "sp"), None),
            P("dp", None),
            P("dp"),
        ),
        out_specs=(P("dp", "sp"), P("dp", "sp")),
        check_vma=False,
    )
```

```python
import functools
import math

import jax
import jax.numpy as jnp
from jax import lax
from jax.experimental import pallas as pl
from jax.experimental.pallas import tpu as pltpu
from jax.sharding import PartitionSpec as P

QUERY_HEADS = 28
KEY_VALUE_HEADS = 4
HEAD_SIZE = 128
HEAD_GROUP = QUERY_HEADS // KEY_VALUE_HEADS
GROUP_WIDTH = HEAD_GROUP * HEAD_SIZE
PAIR = 2
DOCS = 8
SOFTMAX_TEMP = 0.02
VMEM_LIMIT = 48 * 1024 * 1024

VMEM = pl.BlockSpec(memory_space=pltpu.VMEM)
HBM = pl.BlockSpec(memory_space=pltpu.HBM)


def segments(lengths_ref, places):
    end = lengths_ref[0, 0]
    segment = (places >= end).astype(jnp.int32)
    for d in range(1, DOCS):
        end = end + lengths_ref[0, d]
        segment = segment + (places >= end).astype(jnp.int32)
    return segment


def group_columns(ref, group):
    width = ref.shape[1] // KEY_VALUE_HEADS
    return ref.at[:, pl.ds(pl.multiple_of(group * width, HEAD_SIZE), width)]


def cut_kernel(k_hbm, v_hbm, k_out, v_out, near_out, k_far_out, v_far_out, sem):
    core = lax.rem(lax.axis_index("sp"), PAIR)
    plans = [(k_hbm, 0, k_out, 0), (k_hbm, 1, k_far_out, 0), (k_hbm, 1, near_out, 0)]
    plans += [(v_hbm, 1, near_out, PAIR), (v_hbm, 0, v_out, 0), (v_hbm, 1, v_far_out, 0)]
    copies = []
    for source, other, target, start in plans:
        for p in range(PAIR):
            first = (start + p) * HEAD_SIZE
            copies.append(
                pltpu.make_async_copy(
                    group_columns(source, PAIR * p + (core ^ other)),
                    target.at[:, first : first + HEAD_SIZE],
                    sem.at[len(copies)],
                )
            )
    for copy in copies:
        copy.start()
    for copy in copies:
        copy.wait()


def plan_kernel(parts, lengths_hbm, pairs_hbm, q_hbm, q_out, bias_ref, doc_ref, partner_ref, lengths_ref, pairs_ref, sem):
    span = q_hbm.shape[0]
    me = lax.axis_index("sp")
    core = lax.rem(me, PAIR)
    small = [
        pltpu.make_async_copy(lengths_hbm, lengths_ref, sem.at[PAIR]),
        pltpu.make_async_copy(pairs_hbm, pairs_ref, sem.at[PAIR + 1]),
    ]
    copies = [
        pltpu.make_async_copy(
            group_columns(q_hbm, PAIR * p + core),
            q_out.at[:, p * GROUP_WIDTH : (p + 1) * GROUP_WIDTH],
            sem.at[p],
        )
        for p in range(PAIR)
    ]
    for copy in small + copies:
        copy.start()
    for copy in small:
        copy.wait()
    doc = lax.broadcasted_iota(jnp.int32, (DOCS, span), 0)
    weight = jnp.zeros((DOCS, span), jnp.float32)
    for d in range(DOCS):
        weight = jnp.where(doc == d, 1.0 / lengths_ref[0, d].astype(jnp.float32), weight)
    row_segments = [
        segments(lengths_ref, (me ^ r) * span + lax.broadcasted_iota(jnp.int32, (span, 1), 0)) for r in range(PAIR)
    ]
    for r in range(parts):
        columns = slice(r * span, (r + 1) * span)
        key_segment = segments(lengths_ref, (me ^ r) * span + lax.broadcasted_iota(jnp.int32, (1, span), 1))
        for t in range(PAIR):
            bias_ref[t * span : (t + 1) * span, columns] = jnp.where(row_segments[t] == key_segment, 0.0, -1e30)
        doc_ref[:, columns] = jnp.where(key_segment == doc, weight, 0.0)
    own = lax.axis_index("dp")
    own_row = lax.broadcasted_iota(jnp.int32, partner_ref.shape, 0)
    own_column = lax.broadcasted_iota(jnp.int32, partner_ref.shape, 1)
    place = jnp.zeros(partner_ref.shape, jnp.int32)
    for d in range(DOCS):
        pair = pairs_ref[d]
        place = jnp.where(own_row == d, ((pair // DOCS) ^ own) * DOCS + lax.rem(pair, DOCS), place)
    partner_ref[...] = jnp.where(own_column == place, 2.0, 0.0)
    for copy in copies:
        copy.wait()


def scores_kernel(bias_ref, q_own, q_near, k_own, near, k_far, k_last, sums_ref):
    core = lax.rem(lax.axis_index("sp"), PAIR)
    scale = HEAD_SIZE ** (-0.5) * math.log2(math.e)
    for p in range(PAIR):
        here = slice(p * HEAD_SIZE, (p + 1) * HEAD_SIZE)
        key_head = jnp.concatenate([k[:, here] for k in (k_own, near, k_far, k_last)], axis=0)
        for h in range(HEAD_GROUP):
            place = (p * HEAD_GROUP + h) * HEAD_SIZE
            beside = pl.multiple_of((PAIR * p + core) * GROUP_WIDTH + h * HEAD_SIZE, HEAD_SIZE)
            total = None
            for t, query in enumerate((q_own[:, place : place + HEAD_SIZE], q_near[:, pl.ds(beside, HEAD_SIZE)])):
                rows = query.shape[0]
                scores = lax.dot_general(
                    query, key_head, (((1,), (1,)), ((), ())), preferred_element_type=jnp.float32
                )
                scores = scores + bias_ref[t * rows : (t + 1) * rows]
                largest = jnp.max(scores, axis=1, keepdims=True)
                weights = jnp.exp2((scores - largest) * scale)
                probs = weights * (1.0 / jnp.sum(weights, axis=1, keepdims=True))
                summed = jnp.sum(probs, axis=0, keepdims=True)
                total = summed if total is None else total + summed
            row = p * HEAD_GROUP + h
            sums_ref[row : row + 1] = total


def values_kernel(sums_ref, doc_ref, v_own, near, v_far, v_last, out_ref, sent_ref):
    for p in range(PAIR):
        here = slice(p * HEAD_SIZE, (p + 1) * HEAD_SIZE)
        beside = (PAIR + p) * HEAD_SIZE
        value_head = jnp.concatenate(
            [v_own[:, here], near[:, beside : beside + HEAD_SIZE], v_far[:, here], v_last[:, here]], axis=0
        )
        rows = range(p * HEAD_GROUP, (p + 1) * HEAD_GROUP)
        spread = jnp.concatenate([sums_ref[row : row + 1] * doc_ref[...] for row in rows], axis=0)
        high = spread.astype(jnp.bfloat16)
        low = (spread - high.astype(jnp.float32)).astype(jnp.bfloat16)
        summed = jnp.dot(high, value_head, preferred_element_type=jnp.float32) + jnp.dot(
            low, value_head, preferred_element_type=jnp.float32
        )
        for h, row in enumerate(rows):
            out_ref[:, row * HEAD_SIZE : (row + 1) * HEAD_SIZE] = summed[h * DOCS : (h + 1) * DOCS]
    sent_ref[...] = out_ref[...].astype(jnp.bfloat16)


def pool_kernel(corner_ref, far_ref, next_ref, own_ref, sent_ref):
    pooled = own_ref[...] + far_ref[...].astype(jnp.float32)
    beside = next_ref[...].astype(jnp.float32) + corner_ref[...].astype(jnp.float32)
    sent_ref[...] = jnp.concatenate([pooled, beside], axis=0).astype(jnp.bfloat16)


def in_order(refs):
    return (refs[-1], refs[0], *refs[-2:0:-1])


def join_kernel(*refs):
    refs[-1][...] = jnp.concatenate([ref[...] for ref in in_order(refs[:-1])], axis=0)


def gram_kernel(*refs):
    every = jnp.concatenate([ref[...] for ref in in_order(refs[:-1])], axis=0)
    refs[-1][...] = lax.dot_general(every, every, (((1,), (1,)), ((), ())), preferred_element_type=jnp.float32)


def grads_kernel(partner_ref, gram_one, gram_two, *refs):
    every_refs, (own_ref, far_ref, emb_ref, grads_ref) = refs[:-4], refs[-4:]
    gram = gram_one[...] + gram_two[...]
    docs = gram.shape[0]
    columns = pl.ds(pl.multiple_of((lax.axis_index("sp") // PAIR) * GROUP_WIDTH, HEAD_SIZE), GROUP_WIDTH)
    row = lax.broadcasted_iota(jnp.int32, (docs, docs), 0)
    column = lax.broadcasted_iota(jnp.int32, (docs, docs), 1)
    diagonal = row == column
    square = jnp.where(diagonal, gram, 0.0)
    inverse_column = lax.rsqrt(jnp.sum(square, axis=1, keepdims=True) + 1e-6)
    inverse_row = lax.rsqrt(jnp.sum(square, axis=0, keepdims=True) + 1e-6)
    cosine = gram * inverse_column * inverse_row
    logits = jnp.where(diagonal, -jnp.inf, cosine * (1.0 / SOFTMAX_TEMP))
    own = logits[:DOCS]
    largest = jnp.max(own, axis=1, keepdims=True)
    weights = jnp.exp(own - largest)
    probs = weights / jnp.sum(weights, axis=1, keepdims=True)
    largest_row = jnp.max(logits, axis=0, keepdims=True)
    total_row = jnp.sum(jnp.exp(logits - largest_row), axis=0, keepdims=True)
    probs = probs + jnp.exp(own - largest_row) / total_row
    both = probs - partner_ref[...]
    along = jnp.sum(both * cosine[:DOCS], axis=1, keepdims=True) * (1.0 / SOFTMAX_TEMP)
    weighted = both * inverse_row * (1.0 / SOFTMAX_TEMP)
    high = weighted.astype(jnp.bfloat16)
    low = (weighted - high.astype(jnp.float32)).astype(jnp.bfloat16)
    every = jnp.concatenate([ref[:, columns] for ref in in_order(every_refs)], axis=0)
    gradient = jnp.dot(high, every, preferred_element_type=jnp.float32) + jnp.dot(
        low, every, preferred_element_type=jnp.float32
    )
    inverse = inverse_column[:DOCS]
    pooled = own_ref[:, columns] + far_ref[:, columns].astype(jnp.float32)
    embeddings = (pooled * inverse).astype(jnp.bfloat16)
    emb_ref[...] = embeddings
    grads_ref[...] = (gradient - embeddings.astype(jnp.float32) * along) * inverse


def call(kernel, out_shape, in_specs, scratch_shapes=(), flops=0, moved=0):
    return pl.pallas_call(
        kernel,
        out_shape=out_shape,
        in_specs=in_specs,
        out_specs=jax.tree.map(lambda _: VMEM, out_shape),
        scratch_shapes=scratch_shapes,
        compiler_params=pltpu.CompilerParams(vmem_limit_bytes=VMEM_LIMIT),
        cost_estimate=pl.CostEstimate(flops=flops, bytes_accessed=moved, transcendentals=0),
    )


def swap(block, axis, size, distance):
    return lax.ppermute(block, axis, [(s, s ^ distance) for s in range(size)])


def gather_pairs(block, axis, size):
    have, blocks = PAIR, [block]
    while have < size:
        if have > PAIR:
            shape = (len(blocks) * block.shape[0], block.shape[1])
            block = call(join_kernel, jax.ShapeDtypeStruct(shape, block.dtype), [VMEM] * len(blocks))(*blocks)
        radix = min(4, size // have)
        blocks = [swap(block, axis, size, r * have) for r in (1, *range(radix - 1, 1, -1))] + [block]
        have *= radix
    return blocks


def per_device(sizes, queries, keys, values, document_lengths, pair_ids):
    replicas, parts = sizes
    tokens, features = queries.shape
    width = features // PAIR
    kv_width = keys.shape[1] // PAIR
    docs = DOCS * replicas
    f32, bf16 = jnp.float32, jnp.bfloat16
    struct = jax.ShapeDtypeStruct
    query_near = swap(queries, "sp", parts, 1)
    near_cut = struct((tokens, kv_width), bf16)
    arguments = [pltpu.with_memory_space_constraint(x, pltpu.HBM) for x in (document_lengths, pair_ids, queries, keys, values)]
    key_own, value_own, near, key_send, value_send = call(
        cut_kernel,
        (near_cut, near_cut, struct((tokens, 2 * kv_width), bf16), near_cut, near_cut),
        [HBM] * 2,
        [pltpu.SemaphoreType.DMA((6 * PAIR,))],
        moved=8 * keys.size,
    )(*arguments[3:])
    query_own, bias, of_doc, partner = call(
        functools.partial(plan_kernel, parts),
        (
            struct((tokens, width), bf16),
            struct((PAIR * tokens, parts * tokens), f32),
            struct((DOCS, parts * tokens), f32),
            struct((DOCS, docs), f32),
        ),
        [HBM] * 3,
        [
            pltpu.SMEM((1, DOCS), jnp.int32),
            pltpu.SMEM((DOCS,), jnp.int32),
            pltpu.SemaphoreType.DMA((PAIR + 2,)),
        ],
        moved=2 * tokens * features,
    )(*arguments[:3])
    near = swap(near, "sp", parts, 1)
    key_far = swap(key_own, "sp", parts, 2)
    key_last = swap(key_send, "sp", parts, 3)
    value_far = swap(value_own, "sp", parts, 2)
    value_last = swap(value_send, "sp", parts, 3)
    sums = call(
        scores_kernel,
        struct((PAIR * HEAD_GROUP, parts * tokens), f32),
        [VMEM] * 7,
        flops=tokens * features * tokens * parts,
        moved=2 * queries.size + 4 * parts * keys.size,
    )(bias, query_own, query_near, key_own, near, key_far, key_last)
    partial, rounded = call(
        values_kernel, (struct((DOCS, width), f32), struct((DOCS, width), bf16)), [VMEM] * 6
    )(sums, of_doc, value_own, near, value_far, value_last)
    corner = swap(rounded, ("dp", "sp"), replicas * parts, parts + 2)
    far = swap(rounded, "sp", parts, 2)
    beside = swap(rounded, "dp", replicas, 1)
    sent = call(pool_kernel, struct((PAIR * DOCS, width), bf16), [VMEM] * 4)(corner, far, beside, partial)
    blocks = gather_pairs(sent, "dp", replicas)
    gram = call(gram_kernel, struct((docs, docs), f32), [VMEM] * len(blocks))(*blocks)
    return call(
        grads_kernel,
        (struct((DOCS, features // parts), bf16), struct((DOCS, features // parts), f32)),
        [VMEM] * (5 + len(blocks)),
    )(partner, gram, swap(gram, "sp", parts, 1), *blocks, partial, far)


def solution(mesh):
    sizes = (mesh.shape["dp"], mesh.shape["sp"])
    return jax.shard_map(
        functools.partial(per_device, sizes),
        mesh=mesh,
        in_specs=(
            P(("dp", "sp"), None),
            P(("dp", "sp"), None),
            P(("dp", "sp"), None),
            P("dp", None),
            P("dp"),
        ),
        out_specs=(P("dp", "sp"), P("dp", "sp")),
        check_vma=False,
    )
```

```python
import functools
import math

import jax
import jax.numpy as jnp
from jax import lax
from jax.experimental import pallas as pl
from jax.experimental.pallas import tpu as pltpu
from jax.sharding import PartitionSpec as P

QUERY_HEADS = 28
KEY_VALUE_HEADS = 4
HEAD_SIZE = 128
HEAD_GROUP = QUERY_HEADS // KEY_VALUE_HEADS
GROUP_WIDTH = HEAD_GROUP * HEAD_SIZE
PAIR = 2
DOCS = 8
SOFTMAX_TEMP = 0.02
VMEM_LIMIT = 48 * 1024 * 1024

VMEM = pl.BlockSpec(memory_space=pltpu.VMEM)
HBM = pl.BlockSpec(memory_space=pltpu.HBM)


def segments(lengths_ref, places):
    end = lengths_ref[0, 0]
    segment = (places >= end).astype(jnp.int32)
    for d in range(1, DOCS):
        end = end + lengths_ref[0, d]
        segment = segment + (places >= end).astype(jnp.int32)
    return segment


def group_columns(ref, group):
    width = ref.shape[1] // KEY_VALUE_HEADS
    return ref.at[:, pl.ds(pl.multiple_of(group * width, HEAD_SIZE), width)]


def cut_kernel(k_hbm, v_hbm, k_out, v_out, near_out, k_far_out, v_far_out, sem):
    core = lax.rem(lax.axis_index("sp"), PAIR)
    plans = [(k_hbm, 0, k_out, 0), (k_hbm, 1, k_far_out, 0), (k_hbm, 1, near_out, 0)]
    plans += [(v_hbm, 1, near_out, PAIR), (v_hbm, 0, v_out, 0), (v_hbm, 1, v_far_out, 0)]
    copies = []
    for source, other, target, start in plans:
        for p in range(PAIR):
            first = (start + p) * HEAD_SIZE
            copies.append(
                pltpu.make_async_copy(
                    group_columns(source, PAIR * p + (core ^ other)),
                    target.at[:, first : first + HEAD_SIZE],
                    sem.at[len(copies)],
                )
            )
    for copy in copies:
        copy.start()
    for copy in copies:
        copy.wait()


def plan_kernel(parts, lengths_hbm, pairs_hbm, q_hbm, q_out, bias_ref, doc_ref, partner_ref, far_ref, lengths_ref, pairs_ref, sem):
    span = q_hbm.shape[0]
    me = lax.axis_index("sp")
    core = lax.rem(me, PAIR)
    small = [
        pltpu.make_async_copy(lengths_hbm, lengths_ref, sem.at[PAIR]),
        pltpu.make_async_copy(pairs_hbm, pairs_ref, sem.at[PAIR + 1]),
    ]
    copies = [
        pltpu.make_async_copy(
            group_columns(q_hbm, PAIR * p + core),
            q_out.at[:, p * GROUP_WIDTH : (p + 1) * GROUP_WIDTH],
            sem.at[p],
        )
        for p in range(PAIR)
    ]
    for copy in small + copies:
        copy.start()
    for copy in small:
        copy.wait()
    doc = lax.broadcasted_iota(jnp.int32, (DOCS, span), 0)
    weight = jnp.zeros((DOCS, span), jnp.float32)
    for d in range(DOCS):
        weight = jnp.where(doc == d, 1.0 / lengths_ref[0, d].astype(jnp.float32), weight)
    row_segments = [
        segments(lengths_ref, (me ^ r) * span + lax.broadcasted_iota(jnp.int32, (span, 1), 0)) for r in range(PAIR)
    ]
    for r in range(parts):
        columns = slice(r * span, (r + 1) * span)
        key_segment = segments(lengths_ref, (me ^ r) * span + lax.broadcasted_iota(jnp.int32, (1, span), 1))
        for t in range(PAIR):
            bias_ref[t * span : (t + 1) * span, columns] = jnp.where(row_segments[t] == key_segment, 0.0, -1e30)
        doc_ref[:, columns] = jnp.where(key_segment == doc, weight, 0.0)
    firsts = [segments(lengths_ref, (me ^ r) * span) for r in range(parts)]
    lasts = [segments(lengths_ref, (me ^ r) * span + span - 1) for r in range(parts)]
    needs = []
    for t in range(PAIR):
        shared = [
            (jnp.maximum(firsts[t], firsts[r]) <= jnp.minimum(lasts[t], lasts[r])).astype(jnp.int32)
            for r in range(PAIR, parts)
        ]
        needs.append((shared[0] + 2 * shared[1]).astype(jnp.float32))
    flag_row = lax.broadcasted_iota(jnp.int32, far_ref.shape, 0)
    far_ref[...] = jnp.where(flag_row == 0, needs[0], needs[1])
    own = lax.axis_index("dp")
    own_row = lax.broadcasted_iota(jnp.int32, partner_ref.shape, 0)
    own_column = lax.broadcasted_iota(jnp.int32, partner_ref.shape, 1)
    place = jnp.zeros(partner_ref.shape, jnp.int32)
    for d in range(DOCS):
        pair = pairs_ref[d]
        place = jnp.where(own_row == d, ((pair // DOCS) ^ own) * DOCS + lax.rem(pair, DOCS), place)
    partner_ref[...] = jnp.where(own_column == place, 2.0, 0.0)
    for copy in copies:
        copy.wait()


def scores_kernel(far_ref, bias_ref, q_own, q_near, k_own, near, k_far, k_last, sums_ref):
    core = lax.rem(lax.axis_index("sp"), PAIR)
    scale = HEAD_SIZE ** (-0.5) * math.log2(math.e)
    blocks = (k_own, near, k_far, k_last)
    span = k_own.shape[0]

    def attend(t, used):
        rows = slice(t * span, (t + 1) * span)
        bias = jnp.concatenate([bias_ref[rows, r * span : (r + 1) * span] for r in used], axis=1)
        for p in range(PAIR):
            here = slice(p * HEAD_SIZE, (p + 1) * HEAD_SIZE)
            key_head = jnp.concatenate([blocks[r][:, here] for r in used], axis=0)
            for h in range(HEAD_GROUP):
                row = p * HEAD_GROUP + h
                if t == 0:
                    query = q_own[:, row * HEAD_SIZE : (row + 1) * HEAD_SIZE]
                else:
                    first = (PAIR * p + core) * GROUP_WIDTH + h * HEAD_SIZE
                    query = q_near[:, pl.ds(pl.multiple_of(first, HEAD_SIZE), HEAD_SIZE)]
                scores = lax.dot_general(
                    query, key_head, (((1,), (1,)), ((), ())), preferred_element_type=jnp.float32
                )
                scores = scores + bias
                largest = jnp.max(scores, axis=1, keepdims=True)
                weights = jnp.exp2((scores - largest) * scale)
                probs = weights * (1.0 / jnp.sum(weights, axis=1, keepdims=True))
                summed = jnp.sum(probs, axis=0, keepdims=True)
                for i, r in enumerate(used):
                    place = (slice(row, row + 1), slice(r * span, (r + 1) * span))
                    sums_ref[place] = sums_ref[place] + summed[:, i * span : (i + 1) * span]

    sums_ref[...] = jnp.zeros_like(sums_ref)
    for t in range(PAIR):
        need = jnp.max(far_ref[t : t + 1])
        for code, used in enumerate(((0, 1), (0, 1, 2), (0, 1, 3), (0, 1, 2, 3))):
            pl.when(need == code)(functools.partial(attend, t, used))


def values_kernel(sums_ref, doc_ref, v_own, near, v_far, v_last, out_ref, sent_ref):
    for p in range(PAIR):
        here = slice(p * HEAD_SIZE, (p + 1) * HEAD_SIZE)
        beside = (PAIR + p) * HEAD_SIZE
        value_head = jnp.concatenate(
            [v_own[:, here], near[:, beside : beside + HEAD_SIZE], v_far[:, here], v_last[:, here]], axis=0
        )
        rows = range(p * HEAD_GROUP, (p + 1) * HEAD_GROUP)
        spread = jnp.concatenate([sums_ref[row : row + 1] * doc_ref[...] for row in rows], axis=0)
        high = spread.astype(jnp.bfloat16)
        low = (spread - high.astype(jnp.float32)).astype(jnp.bfloat16)
        summed = jnp.dot(high, value_head, preferred_element_type=jnp.float32) + jnp.dot(
            low, value_head, preferred_element_type=jnp.float32
        )
        for h, row in enumerate(rows):
            out_ref[:, row * HEAD_SIZE : (row + 1) * HEAD_SIZE] = summed[h * DOCS : (h + 1) * DOCS]
    sent_ref[...] = out_ref[...].astype(jnp.bfloat16)


def pool_kernel(corner_ref, far_ref, next_ref, own_ref, sent_ref):
    pooled = own_ref[...] + far_ref[...].astype(jnp.float32)
    beside = next_ref[...].astype(jnp.float32) + corner_ref[...].astype(jnp.float32)
    sent_ref[...] = jnp.concatenate([pooled, beside], axis=0).astype(jnp.bfloat16)


def in_order(refs):
    return (refs[-1], refs[0], *refs[-2:0:-1])


def join_kernel(*refs):
    refs[-1][...] = jnp.concatenate([ref[...] for ref in in_order(refs[:-1])], axis=0)


def gram_kernel(*refs):
    every = jnp.concatenate([ref[...] for ref in in_order(refs[:-1])], axis=0)
    refs[-1][...] = lax.dot_general(every, every, (((1,), (1,)), ((), ())), preferred_element_type=jnp.float32)


def grads_kernel(partner_ref, gram_one, gram_two, *refs):
    every_refs, (own_ref, far_ref, emb_ref, grads_ref) = refs[:-4], refs[-4:]
    gram = gram_one[...] + gram_two[...]
    docs = gram.shape[0]
    columns = pl.ds(pl.multiple_of((lax.axis_index("sp") // PAIR) * GROUP_WIDTH, HEAD_SIZE), GROUP_WIDTH)
    row = lax.broadcasted_iota(jnp.int32, (docs, docs), 0)
    column = lax.broadcasted_iota(jnp.int32, (docs, docs), 1)
    diagonal = row == column
    square = jnp.where(diagonal, gram, 0.0)
    inverse_column = lax.rsqrt(jnp.sum(square, axis=1, keepdims=True) + 1e-6)
    inverse_row = lax.rsqrt(jnp.sum(square, axis=0, keepdims=True) + 1e-6)
    cosine = gram * inverse_column * inverse_row
    logits = jnp.where(diagonal, -jnp.inf, cosine * (1.0 / SOFTMAX_TEMP))
    own = logits[:DOCS]
    largest = jnp.max(own, axis=1, keepdims=True)
    weights = jnp.exp(own - largest)
    probs = weights / jnp.sum(weights, axis=1, keepdims=True)
    largest_row = jnp.max(logits, axis=0, keepdims=True)
    total_row = jnp.sum(jnp.exp(logits - largest_row), axis=0, keepdims=True)
    probs = probs + jnp.exp(own - largest_row) / total_row
    both = probs - partner_ref[...]
    along = jnp.sum(both * cosine[:DOCS], axis=1, keepdims=True) * (1.0 / SOFTMAX_TEMP)
    weighted = both * inverse_row * (1.0 / SOFTMAX_TEMP)
    high = weighted.astype(jnp.bfloat16)
    low = (weighted - high.astype(jnp.float32)).astype(jnp.bfloat16)
    every = jnp.concatenate([ref[:, columns] for ref in in_order(every_refs)], axis=0)
    gradient = jnp.dot(high, every, preferred_element_type=jnp.float32) + jnp.dot(
        low, every, preferred_element_type=jnp.float32
    )
    inverse = inverse_column[:DOCS]
    pooled = own_ref[:, columns] + far_ref[:, columns].astype(jnp.float32)
    embeddings = (pooled * inverse).astype(jnp.bfloat16)
    emb_ref[...] = embeddings
    grads_ref[...] = (gradient - embeddings.astype(jnp.float32) * along) * inverse


def call(kernel, out_shape, in_specs, scratch_shapes=(), flops=0, moved=0):
    return pl.pallas_call(
        kernel,
        out_shape=out_shape,
        in_specs=in_specs,
        out_specs=jax.tree.map(lambda _: VMEM, out_shape),
        scratch_shapes=scratch_shapes,
        compiler_params=pltpu.CompilerParams(vmem_limit_bytes=VMEM_LIMIT),
        cost_estimate=pl.CostEstimate(flops=flops, bytes_accessed=moved, transcendentals=0),
    )


def swap(block, axis, size, distance):
    return lax.ppermute(block, axis, [(s, s ^ distance) for s in range(size)])


def gather_pairs(block, axis, size):
    have, blocks = PAIR, [block]
    while have < size:
        if have > PAIR:
            shape = (len(blocks) * block.shape[0], block.shape[1])
            block = call(join_kernel, jax.ShapeDtypeStruct(shape, block.dtype), [VMEM] * len(blocks))(*blocks)
        radix = min(4, size // have)
        blocks = [swap(block, axis, size, r * have) for r in (1, *range(radix - 1, 1, -1))] + [block]
        have *= radix
    return blocks


def per_device(sizes, queries, keys, values, document_lengths, pair_ids):
    replicas, parts = sizes
    tokens, features = queries.shape
    width = features // PAIR
    kv_width = keys.shape[1] // PAIR
    docs = DOCS * replicas
    f32, bf16 = jnp.float32, jnp.bfloat16
    struct = jax.ShapeDtypeStruct
    query_near = swap(queries, "sp", parts, 1)
    near_cut = struct((tokens, kv_width), bf16)
    arguments = [pltpu.with_memory_space_constraint(x, pltpu.HBM) for x in (document_lengths, pair_ids, queries, keys, values)]
    key_own, value_own, near, key_send, value_send = call(
        cut_kernel,
        (near_cut, near_cut, struct((tokens, 2 * kv_width), bf16), near_cut, near_cut),
        [HBM] * 2,
        [pltpu.SemaphoreType.DMA((6 * PAIR,))],
        moved=8 * keys.size,
    )(*arguments[3:])
    query_own, bias, of_doc, partner, far_needs = call(
        functools.partial(plan_kernel, parts),
        (
            struct((tokens, width), bf16),
            struct((PAIR * tokens, parts * tokens), f32),
            struct((DOCS, parts * tokens), f32),
            struct((DOCS, docs), f32),
            struct((8, 128), f32),
        ),
        [HBM] * 3,
        [
            pltpu.SMEM((1, DOCS), jnp.int32),
            pltpu.SMEM((DOCS,), jnp.int32),
            pltpu.SemaphoreType.DMA((PAIR + 2,)),
        ],
        moved=2 * tokens * features,
    )(*arguments[:3])
    near = swap(near, "sp", parts, 1)
    key_far = swap(key_own, "sp", parts, 2)
    key_last = swap(key_send, "sp", parts, 3)
    value_send, value_to_far, near = lax.optimization_barrier((value_send, value_own, near))
    value_far = swap(value_to_far, "sp", parts, 2)
    value_last = swap(value_send, "sp", parts, 3)
    sums = call(
        scores_kernel,
        struct((PAIR * HEAD_GROUP, parts * tokens), f32),
        [VMEM] * 8,
        flops=tokens * features * tokens * parts,
        moved=2 * queries.size + 4 * parts * keys.size,
    )(far_needs, bias, query_own, query_near, key_own, near, key_far, key_last)
    partial, rounded = call(
        values_kernel, (struct((DOCS, width), f32), struct((DOCS, width), bf16)), [VMEM] * 6
    )(sums, of_doc, value_own, near, value_far, value_last)
    corner = swap(rounded, ("dp", "sp"), replicas * parts, parts + 2)
    far = swap(rounded, "sp", parts, 2)
    beside = swap(rounded, "dp", replicas, 1)
    sent = call(pool_kernel, struct((PAIR * DOCS, width), bf16), [VMEM] * 4)(corner, far, beside, partial)
    blocks = gather_pairs(sent, "dp", replicas)
    gram = call(gram_kernel, struct((docs, docs), f32), [VMEM] * len(blocks))(*blocks)
    return call(
        grads_kernel,
        (struct((DOCS, features // parts), bf16), struct((DOCS, features // parts), f32)),
        [VMEM] * (5 + len(blocks)),
    )(partner, gram, swap(gram, "sp", parts, 1), *blocks, partial, far)


def solution(mesh):
    sizes = (mesh.shape["dp"], mesh.shape["sp"])
    return jax.shard_map(
        functools.partial(per_device, sizes),
        mesh=mesh,
        in_specs=(
            P(("dp", "sp"), None),
            P(("dp", "sp"), None),
            P(("dp", "sp"), None),
            P("dp", None),
            P("dp"),
        ),
        out_specs=(P("dp", "sp"), P("dp", "sp")),
        check_vma=False,
    )
```

```python
import functools
import math

import jax
import jax.numpy as jnp
from jax import lax
from jax.experimental import pallas as pl
from jax.experimental.pallas import tpu as pltpu
from jax.sharding import PartitionSpec as P

QUERY_HEADS = 28
KEY_VALUE_HEADS = 4
HEAD_SIZE = 128
HEAD_GROUP = QUERY_HEADS // KEY_VALUE_HEADS
GROUP_WIDTH = HEAD_GROUP * HEAD_SIZE
PAIR = 2
DOCS = 8
SOFTMAX_TEMP = 0.02
VMEM_LIMIT = 48 * 1024 * 1024

VMEM = pl.BlockSpec(memory_space=pltpu.VMEM)
HBM = pl.BlockSpec(memory_space=pltpu.HBM)


def segments(lengths_ref, places):
    end = lengths_ref[0, 0]
    segment = (places >= end).astype(jnp.int32)
    for d in range(1, DOCS):
        end = end + lengths_ref[0, d]
        segment = segment + (places >= end).astype(jnp.int32)
    return segment


def plan_kernel(parts, lengths_hbm, pairs_hbm, q_hbm, k_hbm, v_hbm, *refs):
    q_out, k_out, v_out, near_out, k_far_out, v_far_out, bias_ref, doc_ref, partner_ref, lengths_ref, pairs_ref, sem, small_sem = refs
    span = k_hbm.shape[0]
    me = lax.axis_index("sp")
    core = lax.rem(me, PAIR)
    small = [
        pltpu.make_async_copy(lengths_hbm, lengths_ref, small_sem.at[0]),
        pltpu.make_async_copy(pairs_hbm, pairs_ref, small_sem.at[1]),
    ]
    for copy in small:
        copy.start()
    copies = []

    def cut(source, other, target, start):
        width = source.shape[1] // KEY_VALUE_HEADS
        for p in range(PAIR):
            first = pl.multiple_of((PAIR * p + (core ^ other)) * width, HEAD_SIZE)
            copies.append(
                pltpu.make_async_copy(
                    source.at[:, pl.ds(first, width)],
                    target.at[:, start + p * width : start + (p + 1) * width],
                    sem.at[len(copies)],
                )
            )

    pair_width = PAIR * HEAD_SIZE
    cut(k_hbm, 0, k_out, 0)
    cut(k_hbm, 1, k_far_out, 0)
    cut(k_hbm, 1, near_out, PAIR * GROUP_WIDTH)
    cut(q_hbm, 1, near_out, 0)
    cut(v_hbm, 1, near_out, PAIR * GROUP_WIDTH + pair_width)
    cut(v_hbm, 0, v_out, 0)
    cut(v_hbm, 1, v_far_out, 0)
    cut(q_hbm, 0, q_out, 0)
    for copy in copies:
        copy.start()
    for copy in small:
        copy.wait()
    doc = lax.broadcasted_iota(jnp.int32, (DOCS, span), 0)
    weight = jnp.zeros((DOCS, span), jnp.float32)
    for d in range(DOCS):
        weight = jnp.where(doc == d, 1.0 / lengths_ref[0, d].astype(jnp.float32), weight)
    row_segments = [
        segments(lengths_ref, (me ^ r) * span + lax.broadcasted_iota(jnp.int32, (span, 1), 0)) for r in range(PAIR)
    ]
    for r in range(parts):
        columns = slice(r * span, (r + 1) * span)
        key_segment = segments(lengths_ref, (me ^ r) * span + lax.broadcasted_iota(jnp.int32, (1, span), 1))
        for t in range(PAIR):
            bias_ref[t * span : (t + 1) * span, columns] = jnp.where(row_segments[t] == key_segment, 0.0, -1e30)
        doc_ref[:, columns] = jnp.where(key_segment == doc, weight, 0.0)
    own = lax.axis_index("dp")
    own_row = lax.broadcasted_iota(jnp.int32, partner_ref.shape, 0)
    own_column = lax.broadcasted_iota(jnp.int32, partner_ref.shape, 1)
    half = partner_ref.shape[1] // (PAIR * DOCS)
    place = jnp.zeros(partner_ref.shape, jnp.int32)
    for d in range(DOCS):
        pair = pairs_ref[d]
        far = (pair // DOCS) ^ own
        block = PAIR * lax.rem(far, half) + far // half
        place = jnp.where(own_row == d, block * DOCS + lax.rem(pair, DOCS), place)
    partner_ref[...] = jnp.where(own_column == place, 2.0, 0.0)
    for copy in copies:
        copy.wait()


def scores_kernel(bias_ref, q_own, k_own, near, k_far, k_last, sums_ref):
    scale = HEAD_SIZE ** (-0.5) * math.log2(math.e)
    for p in range(PAIR):
        here = slice(p * HEAD_SIZE, (p + 1) * HEAD_SIZE)
        beside = PAIR * GROUP_WIDTH + p * HEAD_SIZE
        key_head = jnp.concatenate(
            [k_own[:, here], near[:, beside : beside + HEAD_SIZE], k_far[:, here], k_last[:, here]], axis=0
        )
        for h in range(HEAD_GROUP):
            place = (p * HEAD_GROUP + h) * HEAD_SIZE
            total = None
            for t, q_ref in enumerate((q_own, near)):
                query = q_ref[:, place : place + HEAD_SIZE]
                rows = query.shape[0]
                scores = lax.dot_general(
                    query, key_head, (((1,), (1,)), ((), ())), preferred_element_type=jnp.float32
                )
                scores = scores + bias_ref[t * rows : (t + 1) * rows]
                largest = jnp.max(scores, axis=1, keepdims=True)
                weights = jnp.exp2((scores - largest) * scale)
                probs = weights * (1.0 / jnp.sum(weights, axis=1, keepdims=True))
                summed = jnp.sum(probs, axis=0, keepdims=True)
                total = summed if total is None else total + summed
            row = p * HEAD_GROUP + h
            sums_ref[row : row + 1] = total


def values_kernel(sums_ref, doc_ref, v_own, near, v_far, v_last, out_ref, sent_ref):
    for p in range(PAIR):
        here = slice(p * HEAD_SIZE, (p + 1) * HEAD_SIZE)
        beside = PAIR * (GROUP_WIDTH + HEAD_SIZE) + p * HEAD_SIZE
        value_head = jnp.concatenate(
            [v_own[:, here], near[:, beside : beside + HEAD_SIZE], v_far[:, here], v_last[:, here]], axis=0
        )
        rows = range(p * HEAD_GROUP, (p + 1) * HEAD_GROUP)
        spread = jnp.concatenate([sums_ref[row : row + 1] * doc_ref[...] for row in rows], axis=0)
        high = spread.astype(jnp.bfloat16)
        low = (spread - high.astype(jnp.float32)).astype(jnp.bfloat16)
        summed = jnp.dot(high, value_head, preferred_element_type=jnp.float32) + jnp.dot(
            low, value_head, preferred_element_type=jnp.float32
        )
        for h, row in enumerate(rows):
            out_ref[:, row * HEAD_SIZE : (row + 1) * HEAD_SIZE] = summed[h * DOCS : (h + 1) * DOCS]
    sent_ref[...] = out_ref[...].astype(jnp.bfloat16)


def pool_kernel(corner_ref, next_ref, far_ref, own_ref, sent_ref):
    pooled = own_ref[...] + far_ref[...].astype(jnp.float32)
    beside = next_ref[...].astype(jnp.float32) + corner_ref[...].astype(jnp.float32)
    sent_ref[...] = jnp.concatenate([pooled, beside], axis=0).astype(jnp.bfloat16)


def in_order(refs):
    return (refs[-1], *refs[-3::-1], refs[-2])


def join_kernel(*refs):
    refs[-1][...] = jnp.concatenate([ref[...] for ref in in_order(refs[:-1])], axis=0)


def gram_kernel(*refs):
    every = jnp.concatenate([ref[...] for ref in in_order(refs[:-1])], axis=0)
    refs[-1][...] = lax.dot_general(every, every, (((1,), (1,)), ((), ())), preferred_element_type=jnp.float32)


def grads_kernel(partner_ref, gram_one, gram_two, *refs):
    every_refs, (own_ref, far_ref, emb_ref, grads_ref) = refs[:-4], refs[-4:]
    gram = gram_one[...] + gram_two[...]
    docs = gram.shape[0]
    columns = pl.ds(pl.multiple_of((lax.axis_index("sp") // PAIR) * GROUP_WIDTH, HEAD_SIZE), GROUP_WIDTH)
    row = lax.broadcasted_iota(jnp.int32, (docs, docs), 0)
    column = lax.broadcasted_iota(jnp.int32, (docs, docs), 1)
    diagonal = row == column
    square = jnp.where(diagonal, gram, 0.0)
    inverse_column = lax.rsqrt(jnp.sum(square, axis=1, keepdims=True) + 1e-6)
    inverse_row = lax.rsqrt(jnp.sum(square, axis=0, keepdims=True) + 1e-6)
    cosine = gram * inverse_column * inverse_row
    logits = jnp.where(diagonal, -jnp.inf, cosine * (1.0 / SOFTMAX_TEMP))
    own = logits[:DOCS]
    largest = jnp.max(own, axis=1, keepdims=True)
    weights = jnp.exp(own - largest)
    probs = weights / jnp.sum(weights, axis=1, keepdims=True)
    largest_row = jnp.max(logits, axis=0, keepdims=True)
    total_row = jnp.sum(jnp.exp(logits - largest_row), axis=0, keepdims=True)
    probs = probs + jnp.exp(own - largest_row) / total_row
    both = probs - partner_ref[...]
    along = jnp.sum(both * cosine[:DOCS], axis=1, keepdims=True) * (1.0 / SOFTMAX_TEMP)
    weighted = both * inverse_row * (1.0 / SOFTMAX_TEMP)
    high = weighted.astype(jnp.bfloat16)
    low = (weighted - high.astype(jnp.float32)).astype(jnp.bfloat16)
    every = jnp.concatenate([ref[:, columns] for ref in in_order(every_refs)], axis=0)
    gradient = jnp.dot(high, every, preferred_element_type=jnp.float32) + jnp.dot(
        low, every, preferred_element_type=jnp.float32
    )
    inverse = inverse_column[:DOCS]
    pooled = own_ref[:, columns] + far_ref[:, columns].astype(jnp.float32)
    embeddings = (pooled * inverse).astype(jnp.bfloat16)
    emb_ref[...] = embeddings
    grads_ref[...] = (gradient - embeddings.astype(jnp.float32) * along) * inverse


def call(kernel, out_shape, in_specs, scratch_shapes=(), flops=0, moved=0):
    return pl.pallas_call(
        kernel,
        out_shape=out_shape,
        in_specs=in_specs,
        out_specs=jax.tree.map(lambda _: VMEM, out_shape),
        scratch_shapes=scratch_shapes,
        compiler_params=pltpu.CompilerParams(vmem_limit_bytes=VMEM_LIMIT),
        cost_estimate=pl.CostEstimate(flops=flops, bytes_accessed=moved, transcendentals=0),
    )


def swap(block, axis, size, distance):
    return lax.ppermute(block, axis, [(s, s ^ distance) for s in range(size)])


def gather_pairs(block, axis, size):
    have, blocks = 1, [block]
    while PAIR * have < size:
        if have > 1:
            shape = (len(blocks) * block.shape[0], block.shape[1])
            block = call(join_kernel, jax.ShapeDtypeStruct(shape, block.dtype), [VMEM] * len(blocks))(*blocks)
        radix = min(4, size // (PAIR * have))
        blocks = [swap(block, axis, size, r * have) for r in (*range(radix - 2, 0, -1), radix - 1)] + [block]
        have *= radix
    return blocks


def per_device(sizes, queries, keys, values, document_lengths, pair_ids):
    replicas, parts = sizes
    tokens, features = queries.shape
    width = features // PAIR
    kv_width = keys.shape[1] // PAIR
    docs = DOCS * replicas
    f32, bf16 = jnp.float32, jnp.bfloat16
    struct = jax.ShapeDtypeStruct
    query_own, key_own, value_own, near, key_send, value_send, bias, of_doc, partner = call(
        functools.partial(plan_kernel, parts),
        (
            struct((tokens, width), bf16),
            struct((tokens, kv_width), bf16),
            struct((tokens, kv_width), bf16),
            struct((tokens, width + 2 * kv_width), bf16),
            struct((tokens, kv_width), bf16),
            struct((tokens, kv_width), bf16),
            struct((PAIR * tokens, parts * tokens), f32),
            struct((DOCS, parts * tokens), f32),
            struct((DOCS, docs), f32),
        ),
        [HBM] * 5,
        [
            pltpu.SMEM((1, DOCS), jnp.int32),
            pltpu.SMEM((DOCS,), jnp.int32),
            pltpu.SemaphoreType.DMA((8 * PAIR,)),
            pltpu.SemaphoreType.DMA((2,)),
        ],
        moved=2 * tokens * features + 4 * keys.size,
    )(*(pltpu.with_memory_space_constraint(x, pltpu.HBM) for x in (document_lengths, pair_ids, queries, keys, values)))
    near = swap(near, "sp", parts, 1)
    value_far = swap(value_own, "sp", parts, 2)
    value_last = swap(value_send, "sp", parts, 3)
    key_far = swap(key_own, "sp", parts, 2)
    key_last = swap(key_send, "sp", parts, 3)
    sums = call(
        scores_kernel,
        struct((PAIR * HEAD_GROUP, parts * tokens), f32),
        [VMEM] * 6,
        flops=tokens * features * tokens * parts,
        moved=2 * queries.size + 4 * parts * keys.size,
    )(bias, query_own, key_own, near, key_far, key_last)
    partial, rounded = call(
        values_kernel, (struct((DOCS, width), f32), struct((DOCS, width), bf16)), [VMEM] * 6
    )(sums, of_doc, value_own, near, value_far, value_last)
    corner = swap(rounded, ("dp", "sp"), replicas * parts, replicas // PAIR * parts + 2)
    far = swap(rounded, "sp", parts, 2)
    beside = swap(rounded, "dp", replicas, replicas // PAIR)
    sent = call(pool_kernel, struct((PAIR * DOCS, width), bf16), [VMEM] * 4)(corner, beside, far, partial)
    blocks = gather_pairs(sent, "dp", replicas)
    gram = call(gram_kernel, struct((docs, docs), f32), [VMEM] * len(blocks))(*blocks)
    return call(
        grads_kernel,
        (struct((DOCS, features // parts), bf16), struct((DOCS, features // parts), f32)),
        [VMEM] * (5 + len(blocks)),
    )(partner, gram, swap(gram, "sp", parts, 1), *blocks, partial, far)


def solution(mesh):
    sizes = (mesh.shape["dp"], mesh.shape["sp"])
    return jax.shard_map(
        functools.partial(per_device, sizes),
        mesh=mesh,
        in_specs=(
            P(("dp", "sp"), None),
            P(("dp", "sp"), None),
            P(("dp", "sp"), None),
            P("dp", None),
            P("dp"),
        ),
        out_specs=(P("dp", "sp"), P("dp", "sp")),
        check_vma=False,
    )
```

```python
import functools
import math

import jax
import jax.numpy as jnp
from jax import lax
from jax.experimental import pallas as pl
from jax.experimental.pallas import tpu as pltpu
from jax.sharding import PartitionSpec as P

QUERY_HEADS = 28
KEY_VALUE_HEADS = 4
HEAD_SIZE = 128
HEAD_GROUP = QUERY_HEADS // KEY_VALUE_HEADS
GROUP_WIDTH = HEAD_GROUP * HEAD_SIZE
PAIR = 2
DOCS = 8
SOFTMAX_TEMP = 0.02
VMEM_LIMIT = 48 * 1024 * 1024

VMEM = pl.BlockSpec(memory_space=pltpu.VMEM)
HBM = pl.BlockSpec(memory_space=pltpu.HBM)


def segments(lengths_ref, places):
    end = lengths_ref[0, 0]
    segment = (places >= end).astype(jnp.int32)
    for d in range(1, DOCS):
        end = end + lengths_ref[0, d]
        segment = segment + (places >= end).astype(jnp.int32)
    return segment


def plan_kernel(parts, lengths_hbm, pairs_hbm, q_hbm, k_hbm, v_hbm, *refs):
    q_out, k_out, v_out, v_far_out, near_out, bias_ref, doc_ref, partner_ref, lengths_ref, pairs_ref, sem, small_sem = refs
    span = k_hbm.shape[0]
    me = lax.axis_index("sp")
    core = lax.rem(me, PAIR)
    small = [
        pltpu.make_async_copy(lengths_hbm, lengths_ref, small_sem.at[0]),
        pltpu.make_async_copy(pairs_hbm, pairs_ref, small_sem.at[1]),
    ]
    for copy in small:
        copy.start()
    copies = []

    def cut(source, other, target, start):
        width = source.shape[1] // KEY_VALUE_HEADS
        for p in range(PAIR):
            first = pl.multiple_of((PAIR * p + (core ^ other)) * width, HEAD_SIZE)
            copies.append(
                pltpu.make_async_copy(
                    source.at[:, pl.ds(first, width)],
                    target.at[:, start + p * width : start + (p + 1) * width],
                    sem.at[len(copies)],
                )
            )

    cut(v_hbm, 0, v_out, 0)
    cut(v_hbm, 1, v_far_out, 0)
    cut(k_hbm, 0, k_out, 0)
    cut(k_hbm, 1, near_out, 0)
    cut(v_hbm, 1, near_out, PAIR * HEAD_SIZE)
    cut(q_hbm, 0, q_out, 0)
    for copy in copies:
        copy.start()
    for copy in small:
        copy.wait()
    doc = lax.broadcasted_iota(jnp.int32, (DOCS, span), 0)
    weight = jnp.zeros((DOCS, span), jnp.float32)
    for d in range(DOCS):
        weight = jnp.where(doc == d, 1.0 / lengths_ref[0, d].astype(jnp.float32), weight)
    row_segments = [
        segments(lengths_ref, (me ^ r) * span + lax.broadcasted_iota(jnp.int32, (span, 1), 0)) for r in range(PAIR)
    ]
    for r in range(parts):
        columns = slice(r * span, (r + 1) * span)
        key_segment = segments(lengths_ref, (me ^ r) * span + lax.broadcasted_iota(jnp.int32, (1, span), 1))
        for t in range(PAIR):
            bias_ref[t * span : (t + 1) * span, columns] = jnp.where(row_segments[t] == key_segment, 0.0, -1e30)
        doc_ref[:, columns] = jnp.where(key_segment == doc, weight, 0.0)
    own = lax.axis_index("dp")
    own_row = lax.broadcasted_iota(jnp.int32, partner_ref.shape, 0)
    own_column = lax.broadcasted_iota(jnp.int32, partner_ref.shape, 1)
    place = jnp.zeros(partner_ref.shape, jnp.int32)
    for d in range(DOCS):
        pair = pairs_ref[d]
        place = jnp.where(own_row == d, ((pair // DOCS) ^ own) * DOCS + lax.rem(pair, DOCS), place)
    partner_ref[...] = jnp.where(own_column == place, 2.0, 0.0)
    for copy in copies:
        copy.wait()


def cut_kernel(k_ref, one_ref, two_ref):
    other = 1 - lax.rem(lax.axis_index("sp"), PAIR)
    for p, ref in enumerate((one_ref, two_ref)):
        ref[...] = k_ref[:, pl.ds(pl.multiple_of((PAIR * p + other) * HEAD_SIZE, HEAD_SIZE), HEAD_SIZE)]


def scores_kernel(bias_ref, q_own, q_near, k_own, near, k_far, last_one, last_two, sums_ref):
    core = lax.rem(lax.axis_index("sp"), PAIR)
    scale = HEAD_SIZE ** (-0.5) * math.log2(math.e)
    for p, last in enumerate((last_one, last_two)):
        here = slice(p * HEAD_SIZE, (p + 1) * HEAD_SIZE)
        group = PAIR * p + core
        there = pl.ds(pl.multiple_of(group * HEAD_SIZE, HEAD_SIZE), HEAD_SIZE)
        key_head = jnp.concatenate([k_own[:, here], near[:, here], k_far[:, there], last[...]], axis=0)
        for h in range(HEAD_GROUP):
            place = (p * HEAD_GROUP + h) * HEAD_SIZE
            beside = pl.multiple_of(group * GROUP_WIDTH + h * HEAD_SIZE, HEAD_SIZE)
            total = None
            for t, query in enumerate((q_own[:, place : place + HEAD_SIZE], q_near[:, pl.ds(beside, HEAD_SIZE)])):
                rows = query.shape[0]
                scores = lax.dot_general(
                    query, key_head, (((1,), (1,)), ((), ())), preferred_element_type=jnp.float32
                )
                scores = scores + bias_ref[t * rows : (t + 1) * rows]
                largest = jnp.max(scores, axis=1, keepdims=True)
                weights = jnp.exp2((scores - largest) * scale)
                probs = weights * (1.0 / jnp.sum(weights, axis=1, keepdims=True))
                summed = jnp.sum(probs, axis=0, keepdims=True)
                total = summed if total is None else total + summed
            row = p * HEAD_GROUP + h
            sums_ref[row : row + 1] = total


def values_kernel(sums_ref, doc_ref, v_own, near, v_far, v_last, out_ref, sent_ref):
    core = lax.rem(lax.axis_index("sp"), PAIR)
    for p in range(PAIR):
        here = slice(p * HEAD_SIZE, (p + 1) * HEAD_SIZE)
        beside = (PAIR + p) * HEAD_SIZE
        value_head = jnp.concatenate(
            [v_own[:, here], near[:, beside : beside + HEAD_SIZE], v_far[:, here], v_last[:, here]], axis=0
        )
        rows = range(p * HEAD_GROUP, (p + 1) * HEAD_GROUP)
        spread = jnp.concatenate([sums_ref[row : row + 1] * doc_ref[...] for row in rows], axis=0)
        high = spread.astype(jnp.bfloat16)
        low = (spread - high.astype(jnp.float32)).astype(jnp.bfloat16)
        summed = jnp.dot(high, value_head, preferred_element_type=jnp.float32) + jnp.dot(
            low, value_head, preferred_element_type=jnp.float32
        )
        for h, row in enumerate(rows):
            out_ref[:, row * HEAD_SIZE : (row + 1) * HEAD_SIZE] = summed[h * DOCS : (h + 1) * DOCS]
    sent_ref[...] = out_ref[...].astype(jnp.bfloat16)


def pool_kernel(corner_ref, far_ref, next_ref, own_ref, sent_ref):
    pooled = own_ref[...] + far_ref[...].astype(jnp.float32)
    beside = next_ref[...].astype(jnp.float32) + corner_ref[...].astype(jnp.float32)
    sent_ref[...] = jnp.concatenate([pooled, beside], axis=0).astype(jnp.bfloat16)


def in_order(refs):
    return refs[::-1]


def join_kernel(*refs):
    refs[-1][...] = jnp.concatenate([ref[...] for ref in in_order(refs[:-1])], axis=0)


def gram_kernel(*refs):
    every = jnp.concatenate([ref[...] for ref in in_order(refs[:-1])], axis=0)
    refs[-1][...] = lax.dot_general(every, every, (((1,), (1,)), ((), ())), preferred_element_type=jnp.float32)


def grads_kernel(partner_ref, gram_one, gram_two, *refs):
    every_refs, (own_ref, far_ref, emb_ref, grads_ref) = refs[:-4], refs[-4:]
    gram = gram_one[...] + gram_two[...]
    docs = gram.shape[0]
    columns = pl.ds(pl.multiple_of((lax.axis_index("sp") // PAIR) * GROUP_WIDTH, HEAD_SIZE), GROUP_WIDTH)
    row = lax.broadcasted_iota(jnp.int32, (docs, docs), 0)
    column = lax.broadcasted_iota(jnp.int32, (docs, docs), 1)
    diagonal = row == column
    square = jnp.where(diagonal, gram, 0.0)
    inverse_column = lax.rsqrt(jnp.sum(square, axis=1, keepdims=True) + 1e-6)
    inverse_row = lax.rsqrt(jnp.sum(square, axis=0, keepdims=True) + 1e-6)
    cosine = gram * inverse_column * inverse_row
    logits = jnp.where(diagonal, -jnp.inf, cosine * (1.0 / SOFTMAX_TEMP))
    own = logits[:DOCS]
    largest = jnp.max(own, axis=1, keepdims=True)
    weights = jnp.exp(own - largest)
    probs = weights / jnp.sum(weights, axis=1, keepdims=True)
    largest_row = jnp.max(logits, axis=0, keepdims=True)
    total_row = jnp.sum(jnp.exp(logits - largest_row), axis=0, keepdims=True)
    probs = probs + jnp.exp(own - largest_row) / total_row
    both = probs - partner_ref[...]
    along = jnp.sum(both * cosine[:DOCS], axis=1, keepdims=True) * (1.0 / SOFTMAX_TEMP)
    weighted = both * inverse_row * (1.0 / SOFTMAX_TEMP)
    high = weighted.astype(jnp.bfloat16)
    low = (weighted - high.astype(jnp.float32)).astype(jnp.bfloat16)
    every = jnp.concatenate([ref[:, columns] for ref in in_order(every_refs)], axis=0)
    gradient = jnp.dot(high, every, preferred_element_type=jnp.float32) + jnp.dot(
        low, every, preferred_element_type=jnp.float32
    )
    inverse = inverse_column[:DOCS]
    pooled = own_ref[:, columns] + far_ref[:, columns].astype(jnp.float32)
    embeddings = (pooled * inverse).astype(jnp.bfloat16)
    emb_ref[...] = embeddings
    grads_ref[...] = (gradient - embeddings.astype(jnp.float32) * along) * inverse


def call(kernel, out_shape, in_specs, scratch_shapes=(), flops=0, moved=0):
    return pl.pallas_call(
        kernel,
        out_shape=out_shape,
        in_specs=in_specs,
        out_specs=jax.tree.map(lambda _: VMEM, out_shape),
        scratch_shapes=scratch_shapes,
        compiler_params=pltpu.CompilerParams(vmem_limit_bytes=VMEM_LIMIT),
        cost_estimate=pl.CostEstimate(flops=flops, bytes_accessed=moved, transcendentals=0),
    )


def swap(block, axis, size, distance):
    return lax.ppermute(block, axis, [(s, s ^ distance) for s in range(size)])


def gather_pairs(block, axis, size):
    have, blocks = PAIR, [block]
    while have < size:
        if have > PAIR:
            shape = (len(blocks) * block.shape[0], block.shape[1])
            block = call(join_kernel, jax.ShapeDtypeStruct(shape, block.dtype), [VMEM] * len(blocks))(*blocks)
        radix = min(4, size // have)
        blocks = [swap(block, axis, size, r * have) for r in range(radix - 1, 0, -1)] + [block]
        have *= radix
    return blocks


def per_device(sizes, queries, keys, values, document_lengths, pair_ids):
    replicas, parts = sizes
    tokens, features = queries.shape
    width = features // PAIR
    kv_width = keys.shape[1] // PAIR
    docs = DOCS * replicas
    f32, bf16 = jnp.float32, jnp.bfloat16
    struct = jax.ShapeDtypeStruct
    key_far, query_near = swap(keys, "sp", parts, 2), swap(queries, "sp", parts, 1)
    arguments = [pltpu.with_memory_space_constraint(x, pltpu.HBM) for x in (pair_ids, queries, keys, values)]
    query_own, key_own, value_own, value_send, near, bias, of_doc, partner = call(
        functools.partial(plan_kernel, parts),
        (
            struct((tokens, width), bf16),
            *(struct((tokens, kv_width), bf16),) * 3,
            struct((tokens, 2 * kv_width), bf16),
            struct((PAIR * tokens, parts * tokens), f32),
            struct((DOCS, parts * tokens), f32),
            struct((DOCS, docs), f32),
        ),
        [HBM] * 5,
        [
            pltpu.SMEM((1, DOCS), jnp.int32),
            pltpu.SMEM((DOCS,), jnp.int32),
            pltpu.SemaphoreType.DMA((6 * PAIR,)),
            pltpu.SemaphoreType.DMA((2,)),
        ],
        moved=2 * tokens * features + 4 * keys.size,
    )(pltpu.with_memory_space_constraint(document_lengths, pltpu.HBM), *arguments)
    near = swap(near, "sp", parts, 1)
    value_far = swap(value_own, "sp", parts, 2)
    value_last = swap(value_send, "sp", parts, 3)
    last = [
        swap(cut, "sp", parts, 1)
        for cut in call(cut_kernel, (struct((tokens, HEAD_SIZE), bf16),) * PAIR, [VMEM])(key_far)
    ]
    sums = call(
        scores_kernel,
        struct((PAIR * HEAD_GROUP, parts * tokens), f32),
        [VMEM] * 8,
        flops=tokens * features * tokens * parts,
        moved=2 * queries.size + 4 * parts * keys.size,
    )(bias, query_own, query_near, key_own, near, key_far, *last)
    partial, rounded = call(
        values_kernel, (struct((DOCS, width), f32), struct((DOCS, width), bf16)), [VMEM] * 6
    )(sums, of_doc, value_own, near, value_far, value_last)
    corner = swap(rounded, ("dp", "sp"), replicas * parts, parts + 2)
    far = swap(rounded, "sp", parts, 2)
    beside = swap(rounded, "dp", replicas, 1)
    sent = call(pool_kernel, struct((PAIR * DOCS, width), bf16), [VMEM] * 4)(corner, far, beside, partial)
    blocks = gather_pairs(sent, "dp", replicas)
    gram = call(gram_kernel, struct((docs, docs), f32), [VMEM] * len(blocks))(*blocks)
    return call(
        grads_kernel,
        (struct((DOCS, features // parts), bf16), struct((DOCS, features // parts), f32)),
        [VMEM] * (5 + len(blocks)),
    )(partner, gram, swap(gram, "sp", parts, 1), *blocks, partial, far)


def solution(mesh):
    sizes = (mesh.shape["dp"], mesh.shape["sp"])
    return jax.shard_map(
        functools.partial(per_device, sizes),
        mesh=mesh,
        in_specs=(
            P(("dp", "sp"), None),
            P(("dp", "sp"), None),
            P(("dp", "sp"), None),
            P("dp", None),
            P("dp"),
        ),
        out_specs=(P("dp", "sp"), P("dp", "sp")),
        check_vma=False,
    )
```

```python
import functools
import math

import jax
import jax.numpy as jnp
from jax import lax
from jax.experimental import pallas as pl
from jax.experimental.pallas import tpu as pltpu
from jax.sharding import PartitionSpec as P

QUERY_HEADS = 28
KEY_VALUE_HEADS = 4
HEAD_SIZE = 128
HEAD_GROUP = QUERY_HEADS // KEY_VALUE_HEADS
GROUP_WIDTH = HEAD_GROUP * HEAD_SIZE
PAIR = 2
DOCS = 8
SOFTMAX_TEMP = 0.02
VMEM_LIMIT = 48 * 1024 * 1024

VMEM = pl.BlockSpec(memory_space=pltpu.VMEM)
HBM = pl.BlockSpec(memory_space=pltpu.HBM)


def segments(lengths_ref, places):
    end = lengths_ref[0, 0]
    segment = (places >= end).astype(jnp.int32)
    for d in range(1, DOCS):
        end = end + lengths_ref[0, d]
        segment = segment + (places >= end).astype(jnp.int32)
    return segment


def plan_kernel(parts, lengths_hbm, pairs_hbm, q_hbm, k_hbm, v_hbm, *refs):
    q_out, k_out, v_out, near_out, k_far_out, v_far_out, bias_ref, doc_ref, partner_ref, lengths_ref, pairs_ref, sem, small_sem = refs
    span = k_hbm.shape[0]
    me = lax.axis_index("sp")
    core = lax.rem(me, PAIR)
    small = [
        pltpu.make_async_copy(lengths_hbm, lengths_ref, small_sem.at[0]),
        pltpu.make_async_copy(pairs_hbm, pairs_ref, small_sem.at[1]),
    ]
    for copy in small:
        copy.start()
    copies = []

    def cut(source, other, target, start):
        width = source.shape[1] // KEY_VALUE_HEADS
        for p in range(PAIR):
            first = pl.multiple_of((PAIR * p + (core ^ other)) * width, HEAD_SIZE)
            copies.append(
                pltpu.make_async_copy(
                    source.at[:, pl.ds(first, width)],
                    target.at[:, start + p * width : start + (p + 1) * width],
                    sem.at[len(copies)],
                )
            )

    pair_width = PAIR * HEAD_SIZE
    cut(k_hbm, 0, k_out, 0)
    cut(k_hbm, 1, k_far_out, 0)
    cut(k_hbm, 1, near_out, PAIR * GROUP_WIDTH)
    cut(q_hbm, 1, near_out, 0)
    cut(v_hbm, 1, near_out, PAIR * GROUP_WIDTH + pair_width)
    cut(v_hbm, 0, v_out, 0)
    cut(v_hbm, 1, v_far_out, 0)
    cut(q_hbm, 0, q_out, 0)
    for copy in copies:
        copy.start()
    for copy in small:
        copy.wait()
    doc = lax.broadcasted_iota(jnp.int32, (DOCS, span), 0)
    weight = jnp.zeros((DOCS, span), jnp.float32)
    for d in range(DOCS):
        weight = jnp.where(doc == d, 1.0 / lengths_ref[0, d].astype(jnp.float32), weight)
    row_segments = [
        segments(lengths_ref, (me ^ r) * span + lax.broadcasted_iota(jnp.int32, (span, 1), 0)) for r in range(PAIR)
    ]
    for r in range(parts):
        columns = slice(r * span, (r + 1) * span)
        key_segment = segments(lengths_ref, (me ^ r) * span + lax.broadcasted_iota(jnp.int32, (1, span), 1))
        for t in range(PAIR):
            bias_ref[t * span : (t + 1) * span, columns] = jnp.where(row_segments[t] == key_segment, 0.0, -1e30)
        doc_ref[:, columns] = jnp.where(key_segment == doc, weight, 0.0)
    own = lax.axis_index("dp")
    own_row = lax.broadcasted_iota(jnp.int32, partner_ref.shape, 0)
    own_column = lax.broadcasted_iota(jnp.int32, partner_ref.shape, 1)
    place = jnp.zeros(partner_ref.shape, jnp.int32)
    for d in range(DOCS):
        pair = pairs_ref[d]
        place = jnp.where(own_row == d, ((pair // DOCS) ^ own) * DOCS + lax.rem(pair, DOCS), place)
    partner_ref[...] = jnp.where(own_column == place, 2.0, 0.0)
    for copy in copies:
        copy.wait()


def scores_kernel(bias_ref, q_own, k_own, near, k_far, k_last, sums_ref):
    scale = HEAD_SIZE ** (-0.5) * math.log2(math.e)
    for p in range(PAIR):
        here = slice(p * HEAD_SIZE, (p + 1) * HEAD_SIZE)
        beside = PAIR * GROUP_WIDTH + p * HEAD_SIZE
        key_head = jnp.concatenate(
            [k_own[:, here], near[:, beside : beside + HEAD_SIZE], k_far[:, here], k_last[:, here]], axis=0
        )
        for h in range(HEAD_GROUP):
            place = (p * HEAD_GROUP + h) * HEAD_SIZE
            total = None
            for t, q_ref in enumerate((q_own, near)):
                query = q_ref[:, place : place + HEAD_SIZE]
                rows = query.shape[0]
                scores = lax.dot_general(
                    query, key_head, (((1,), (1,)), ((), ())), preferred_element_type=jnp.float32
                )
                scores = scores + bias_ref[t * rows : (t + 1) * rows]
                largest = jnp.max(scores, axis=1, keepdims=True)
                weights = jnp.exp2((scores - largest) * scale)
                probs = weights * (1.0 / jnp.sum(weights, axis=1, keepdims=True))
                summed = jnp.sum(probs, axis=0, keepdims=True)
                total = summed if total is None else total + summed
            row = p * HEAD_GROUP + h
            sums_ref[row : row + 1] = total


def values_kernel(sums_ref, doc_ref, v_own, near, v_far, v_last, out_ref, sent_ref):
    for p in range(PAIR):
        here = slice(p * HEAD_SIZE, (p + 1) * HEAD_SIZE)
        beside = PAIR * (GROUP_WIDTH + HEAD_SIZE) + p * HEAD_SIZE
        value_head = jnp.concatenate(
            [v_own[:, here], near[:, beside : beside + HEAD_SIZE], v_far[:, here], v_last[:, here]], axis=0
        )
        rows = range(p * HEAD_GROUP, (p + 1) * HEAD_GROUP)
        spread = jnp.concatenate([sums_ref[row : row + 1] * doc_ref[...] for row in rows], axis=0)
        high = spread.astype(jnp.bfloat16)
        low = (spread - high.astype(jnp.float32)).astype(jnp.bfloat16)
        summed = jnp.dot(high, value_head, preferred_element_type=jnp.float32) + jnp.dot(
            low, value_head, preferred_element_type=jnp.float32
        )
        for h, row in enumerate(rows):
            out_ref[:, row * HEAD_SIZE : (row + 1) * HEAD_SIZE] = summed[h * DOCS : (h + 1) * DOCS]
    sent_ref[...] = out_ref[...].astype(jnp.bfloat16)


def pool_kernel(corner_ref, far_ref, next_ref, own_ref, sent_ref):
    pooled = own_ref[...] + far_ref[...].astype(jnp.float32)
    beside = next_ref[...].astype(jnp.float32) + corner_ref[...].astype(jnp.float32)
    sent_ref[...] = jnp.concatenate([pooled, beside], axis=0).astype(jnp.bfloat16)


def in_order(refs):
    return (refs[-1], *refs[-3::-1], refs[-2])


def join_kernel(*refs):
    refs[-1][...] = jnp.concatenate([ref[...] for ref in in_order(refs[:-1])], axis=0)


def gram_kernel(*refs):
    every = jnp.concatenate([ref[...] for ref in in_order(refs[:-1])], axis=0)
    refs[-1][...] = lax.dot_general(every, every, (((1,), (1,)), ((), ())), preferred_element_type=jnp.float32)


def grads_kernel(partner_ref, gram_one, gram_two, *refs):
    every_refs, (own_ref, far_ref, emb_ref, grads_ref) = refs[:-4], refs[-4:]
    gram = gram_one[...] + gram_two[...]
    docs = gram.shape[0]
    columns = pl.ds(pl.multiple_of((lax.axis_index("sp") // PAIR) * GROUP_WIDTH, HEAD_SIZE), GROUP_WIDTH)
    row = lax.broadcasted_iota(jnp.int32, (docs, docs), 0)
    column = lax.broadcasted_iota(jnp.int32, (docs, docs), 1)
    diagonal = row == column
    square = jnp.where(diagonal, gram, 0.0)
    inverse_column = lax.rsqrt(jnp.sum(square, axis=1, keepdims=True) + 1e-6)
    inverse_row = lax.rsqrt(jnp.sum(square, axis=0, keepdims=True) + 1e-6)
    cosine = gram * inverse_column * inverse_row
    weights = jnp.where(diagonal, 0.0, jnp.exp(cosine * (1.0 / SOFTMAX_TEMP)))
    own = weights[:DOCS]
    total = 1.0 / jnp.sum(own, axis=1, keepdims=True) + 1.0 / jnp.sum(weights, axis=0, keepdims=True)
    both = own * total - partner_ref[...]
    along = jnp.sum(both * cosine[:DOCS], axis=1, keepdims=True) * (1.0 / SOFTMAX_TEMP)
    weighted = both * inverse_row * (1.0 / SOFTMAX_TEMP)
    high = weighted.astype(jnp.bfloat16)
    low = (weighted - high.astype(jnp.float32)).astype(jnp.bfloat16)
    every = jnp.concatenate([ref[:, columns] for ref in in_order(every_refs)], axis=0)
    gradient = jnp.dot(high, every, preferred_element_type=jnp.float32) + jnp.dot(
        low, every, preferred_element_type=jnp.float32
    )
    inverse = inverse_column[:DOCS]
    pooled = own_ref[:, columns] + far_ref[:, columns].astype(jnp.float32)
    embeddings = (pooled * inverse).astype(jnp.bfloat16)
    emb_ref[...] = embeddings
    grads_ref[...] = (gradient - embeddings.astype(jnp.float32) * along) * inverse


def call(kernel, out_shape, in_specs, scratch_shapes=(), flops=0, moved=0):
    return pl.pallas_call(
        kernel,
        out_shape=out_shape,
        in_specs=in_specs,
        out_specs=jax.tree.map(lambda _: VMEM, out_shape),
        scratch_shapes=scratch_shapes,
        compiler_params=pltpu.CompilerParams(vmem_limit_bytes=VMEM_LIMIT),
        cost_estimate=pl.CostEstimate(flops=flops, bytes_accessed=moved, transcendentals=0),
    )


def swap(block, axis, size, distance):
    return lax.ppermute(block, axis, [(s, s ^ distance) for s in range(size)])


def gather_pairs(block, axis, size):
    have, blocks = PAIR, [block]
    while have < size:
        if have > PAIR:
            shape = (len(blocks) * block.shape[0], block.shape[1])
            block = call(join_kernel, jax.ShapeDtypeStruct(shape, block.dtype), [VMEM] * len(blocks))(*blocks)
        radix = min(4, size // have)
        blocks = [swap(block, axis, size, r * have) for r in (*range(radix - 2, 0, -1), radix - 1)] + [block]
        have *= radix
    return blocks


def per_device(sizes, queries, keys, values, document_lengths, pair_ids):
    replicas, parts = sizes
    tokens, features = queries.shape
    width = features // PAIR
    kv_width = keys.shape[1] // PAIR
    docs = DOCS * replicas
    f32, bf16 = jnp.float32, jnp.bfloat16
    struct = jax.ShapeDtypeStruct
    query_own, key_own, value_own, near, key_send, value_send, bias, of_doc, partner = call(
        functools.partial(plan_kernel, parts),
        (
            struct((tokens, width), bf16),
            struct((tokens, kv_width), bf16),
            struct((tokens, kv_width), bf16),
            struct((tokens, width + 2 * kv_width), bf16),
            struct((tokens, kv_width), bf16),
            struct((tokens, kv_width), bf16),
            struct((PAIR * tokens, parts * tokens), f32),
            struct((DOCS, parts * tokens), f32),
            struct((DOCS, docs), f32),
        ),
        [HBM] * 5,
        [
            pltpu.SMEM((1, DOCS), jnp.int32),
            pltpu.SMEM((DOCS,), jnp.int32),
            pltpu.SemaphoreType.DMA((8 * PAIR,)),
            pltpu.SemaphoreType.DMA((2,)),
        ],
        moved=2 * tokens * features + 4 * keys.size,
    )(*(pltpu.with_memory_space_constraint(x, pltpu.HBM) for x in (document_lengths, pair_ids, queries, keys, values)))
    near = swap(near, "sp", parts, 1)
    value_far = swap(value_own, "sp", parts, 2)
    value_last = swap(value_send, "sp", parts, 3)
    key_far = swap(key_own, "sp", parts, 2)
    key_last = swap(key_send, "sp", parts, 3)
    sums = call(
        scores_kernel,
        struct((PAIR * HEAD_GROUP, parts * tokens), f32),
        [VMEM] * 6,
        flops=tokens * features * tokens * parts,
        moved=2 * queries.size + 4 * parts * keys.size,
    )(bias, query_own, key_own, near, key_far, key_last)
    partial, rounded = call(
        values_kernel, (struct((DOCS, width), f32), struct((DOCS, width), bf16)), [VMEM] * 6
    )(sums, of_doc, value_own, near, value_far, value_last)
    corner = swap(rounded, ("dp", "sp"), replicas * parts, parts + 2)
    far = swap(rounded, "sp", parts, 2)
    beside = swap(rounded, "dp", replicas, 1)
    sent = call(pool_kernel, struct((PAIR * DOCS, width), bf16), [VMEM] * 4)(corner, far, beside, partial)
    blocks = gather_pairs(sent, "dp", replicas)
    gram = call(gram_kernel, struct((docs, docs), f32), [VMEM] * len(blocks))(*blocks)
    return call(
        grads_kernel,
        (struct((DOCS, features // parts), bf16), struct((DOCS, features // parts), f32)),
        [VMEM] * (5 + len(blocks)),
    )(partner, gram, swap(gram, "sp", parts, 1), *blocks, partial, far)


def solution(mesh):
    sizes = (mesh.shape["dp"], mesh.shape["sp"])
    return jax.shard_map(
        functools.partial(per_device, sizes),
        mesh=mesh,
        in_specs=(
            P(("dp", "sp"), None),
            P(("dp", "sp"), None),
            P(("dp", "sp"), None),
            P("dp", None),
            P("dp"),
        ),
        out_specs=(P("dp", "sp"), P("dp", "sp")),
        check_vma=False,
    )
```

```python
import functools
import math

import jax
import jax.numpy as jnp
from jax import lax
from jax.experimental import pallas as pl
from jax.experimental.pallas import tpu as pltpu
from jax.sharding import PartitionSpec as P

QUERY_HEADS = 28
KEY_VALUE_HEADS = 4
HEAD_SIZE = 128
HEAD_GROUP = QUERY_HEADS // KEY_VALUE_HEADS
GROUP_WIDTH = HEAD_GROUP * HEAD_SIZE
PAIR = 2
DOCS = 8
SOFTMAX_TEMP = 0.02
VMEM_LIMIT = 48 * 1024 * 1024

VMEM = pl.BlockSpec(memory_space=pltpu.VMEM)
HBM = pl.BlockSpec(memory_space=pltpu.HBM)


def segments(lengths_ref, places):
    end = lengths_ref[0, 0]
    segment = (places >= end).astype(jnp.int32)
    for d in range(1, DOCS):
        end = end + lengths_ref[0, d]
        segment = segment + (places >= end).astype(jnp.int32)
    return segment


def plan_kernel(parts, lengths_hbm, pairs_hbm, q_hbm, k_hbm, v_hbm, *refs):
    q_out, k_out, v_out, v_far_out, near_out, bias_ref, doc_ref, partner_ref, lengths_ref, pairs_ref, sem, small_sem = refs
    span = k_hbm.shape[0]
    me = lax.axis_index("sp")
    core = lax.rem(me, PAIR)
    small = [
        pltpu.make_async_copy(lengths_hbm, lengths_ref, small_sem.at[0]),
        pltpu.make_async_copy(pairs_hbm, pairs_ref, small_sem.at[1]),
    ]
    for copy in small:
        copy.start()
    copies = []

    def cut(source, other, target, start):
        width = source.shape[1] // KEY_VALUE_HEADS
        for p in range(PAIR):
            first = pl.multiple_of((PAIR * p + (core ^ other)) * width, HEAD_SIZE)
            copies.append(
                pltpu.make_async_copy(
                    source.at[:, pl.ds(first, width)],
                    target.at[:, start + p * width : start + (p + 1) * width],
                    sem.at[len(copies)],
                )
            )

    cut(v_hbm, 0, v_out, 0)
    cut(v_hbm, 1, v_far_out, 0)
    cut(k_hbm, 0, k_out, 0)
    cut(k_hbm, 1, near_out, 0)
    cut(v_hbm, 1, near_out, PAIR * HEAD_SIZE)
    cut(q_hbm, 0, q_out, 0)
    for copy in copies:
        copy.start()
    for copy in small:
        copy.wait()
    doc = lax.broadcasted_iota(jnp.int32, (DOCS, span), 0)
    weight = jnp.zeros((DOCS, span), jnp.float32)
    for d in range(DOCS):
        weight = jnp.where(doc == d, 1.0 / lengths_ref[0, d].astype(jnp.float32), weight)
    row_segments = [
        segments(lengths_ref, (me ^ r) * span + lax.broadcasted_iota(jnp.int32, (span, 1), 0)) for r in range(PAIR)
    ]
    for r in range(parts):
        columns = slice(r * span, (r + 1) * span)
        key_segment = segments(lengths_ref, (me ^ r) * span + lax.broadcasted_iota(jnp.int32, (1, span), 1))
        for t in range(PAIR):
            bias_ref[t * span : (t + 1) * span, columns] = jnp.where(row_segments[t] == key_segment, 0.0, -1e30)
        doc_ref[:, columns] = jnp.where(key_segment == doc, weight, 0.0)
    own = lax.axis_index("dp")
    own_row = lax.broadcasted_iota(jnp.int32, partner_ref.shape, 0)
    own_column = lax.broadcasted_iota(jnp.int32, partner_ref.shape, 1)
    place = jnp.zeros(partner_ref.shape, jnp.int32)
    for d in range(DOCS):
        pair = pairs_ref[d]
        place = jnp.where(own_row == d, ((pair // DOCS) ^ own) * DOCS + lax.rem(pair, DOCS), place)
    partner_ref[...] = jnp.where(own_column == place, 2.0, 0.0)
    for copy in copies:
        copy.wait()


def cut_kernel(k_ref, one_ref, two_ref):
    other = 1 - lax.rem(lax.axis_index("sp"), PAIR)
    for p, ref in enumerate((one_ref, two_ref)):
        ref[...] = k_ref[:, pl.ds(pl.multiple_of((PAIR * p + other) * HEAD_SIZE, HEAD_SIZE), HEAD_SIZE)]


def scores_kernel(bias_ref, q_own, q_near, k_own, near, k_far, last_one, last_two, sums_ref):
    core = lax.rem(lax.axis_index("sp"), PAIR)
    scale = HEAD_SIZE ** (-0.5) * math.log2(math.e)
    span = k_own.shape[0]
    for p, last in enumerate((last_one, last_two)):
        here = slice(p * HEAD_SIZE, (p + 1) * HEAD_SIZE)
        group = PAIR * p + core
        there = pl.ds(pl.multiple_of(group * HEAD_SIZE, HEAD_SIZE), HEAD_SIZE)
        key_head = jnp.concatenate([k_own[:, here], near[:, here], k_far[:, there], last[...]], axis=0)

        def one_head(h, carry):
            place = pl.ds(pl.multiple_of((p * HEAD_GROUP + h) * HEAD_SIZE, HEAD_SIZE), HEAD_SIZE)
            beside = pl.ds(pl.multiple_of((group * HEAD_GROUP + h) * HEAD_SIZE, HEAD_SIZE), HEAD_SIZE)
            total = 0.0
            for t, query in enumerate((q_own[:, place], q_near[:, beside])):
                scores = lax.dot_general(
                    query, key_head, (((1,), (1,)), ((), ())), preferred_element_type=jnp.float32
                )
                scores = scores + bias_ref[t * span : (t + 1) * span]
                largest = jnp.max(scores, axis=1, keepdims=True)
                weights = jnp.exp2((scores - largest) * scale)
                probs = weights * (1.0 / jnp.sum(weights, axis=1, keepdims=True))
                total = total + jnp.sum(probs, axis=0, keepdims=True)
            sums_ref[p * HEAD_GROUP + h] = total
            return carry

        lax.fori_loop(0, HEAD_GROUP, one_head, 0)


def values_kernel(sums_ref, doc_ref, v_own, near, v_far, v_last, out_ref, sent_ref):
    core = lax.rem(lax.axis_index("sp"), PAIR)
    for p in range(PAIR):
        here = slice(p * HEAD_SIZE, (p + 1) * HEAD_SIZE)
        beside = (PAIR + p) * HEAD_SIZE
        value_head = jnp.concatenate(
            [v_own[:, here], near[:, beside : beside + HEAD_SIZE], v_far[:, here], v_last[:, here]], axis=0
        )
        rows = range(p * HEAD_GROUP, (p + 1) * HEAD_GROUP)
        spread = jnp.concatenate([sums_ref[row] * doc_ref[...] for row in rows], axis=0)
        high = spread.astype(jnp.bfloat16)
        low = (spread - high.astype(jnp.float32)).astype(jnp.bfloat16)
        summed = jnp.dot(high, value_head, preferred_element_type=jnp.float32) + jnp.dot(
            low, value_head, preferred_element_type=jnp.float32
        )
        for h, row in enumerate(rows):
            out_ref[:, row * HEAD_SIZE : (row + 1) * HEAD_SIZE] = summed[h * DOCS : (h + 1) * DOCS]
    sent_ref[...] = out_ref[...].astype(jnp.bfloat16)


def pool_kernel(corner_ref, far_ref, next_ref, own_ref, sent_ref):
    pooled = own_ref[...] + far_ref[...].astype(jnp.float32)
    beside = next_ref[...].astype(jnp.float32) + corner_ref[...].astype(jnp.float32)
    sent_ref[...] = jnp.concatenate([pooled, beside], axis=0).astype(jnp.bfloat16)


def in_order(refs):
    return refs[::-1]


def join_kernel(*refs):
    refs[-1][...] = jnp.concatenate([ref[...] for ref in in_order(refs[:-1])], axis=0)


def gram_kernel(*refs):
    every = jnp.concatenate([ref[...] for ref in in_order(refs[:-1])], axis=0)
    refs[-1][...] = lax.dot_general(every, every, (((1,), (1,)), ((), ())), preferred_element_type=jnp.float32)


def grads_kernel(partner_ref, gram_one, gram_two, *refs):
    every_refs, (own_ref, far_ref, emb_ref, grads_ref) = refs[:-4], refs[-4:]
    gram = gram_one[...] + gram_two[...]
    docs = gram.shape[0]
    columns = pl.ds(pl.multiple_of((lax.axis_index("sp") // PAIR) * GROUP_WIDTH, HEAD_SIZE), GROUP_WIDTH)
    row = lax.broadcasted_iota(jnp.int32, (docs, docs), 0)
    column = lax.broadcasted_iota(jnp.int32, (docs, docs), 1)
    diagonal = row == column
    square = jnp.where(diagonal, gram, 0.0)
    inverse_column = lax.rsqrt(jnp.sum(square, axis=1, keepdims=True) + 1e-6)
    inverse_row = lax.rsqrt(jnp.sum(square, axis=0, keepdims=True) + 1e-6)
    cosine = gram * inverse_column * inverse_row
    weights = jnp.where(diagonal, 0.0, jnp.exp(cosine * (1.0 / SOFTMAX_TEMP)))
    own = weights[:DOCS]
    total = 1.0 / jnp.sum(own, axis=1, keepdims=True) + 1.0 / jnp.sum(weights, axis=0, keepdims=True)
    both = own * total - partner_ref[...]
    along = jnp.sum(both * cosine[:DOCS], axis=1, keepdims=True) * (1.0 / SOFTMAX_TEMP)
    weighted = both * inverse_row * (1.0 / SOFTMAX_TEMP)
    high = weighted.astype(jnp.bfloat16)
    low = (weighted - high.astype(jnp.float32)).astype(jnp.bfloat16)
    every = jnp.concatenate([ref[:, columns] for ref in in_order(every_refs)], axis=0)
    gradient = jnp.dot(high, every, preferred_element_type=jnp.float32) + jnp.dot(
        low, every, preferred_element_type=jnp.float32
    )
    inverse = inverse_column[:DOCS]
    pooled = own_ref[:, columns] + far_ref[:, columns].astype(jnp.float32)
    embeddings = (pooled * inverse).astype(jnp.bfloat16)
    emb_ref[...] = embeddings
    grads_ref[...] = (gradient - embeddings.astype(jnp.float32) * along) * inverse


def call(kernel, out_shape, in_specs, scratch_shapes=(), flops=0, moved=0):
    return pl.pallas_call(
        kernel,
        out_shape=out_shape,
        in_specs=in_specs,
        out_specs=jax.tree.map(lambda _: VMEM, out_shape),
        scratch_shapes=scratch_shapes,
        compiler_params=pltpu.CompilerParams(vmem_limit_bytes=VMEM_LIMIT),
        cost_estimate=pl.CostEstimate(flops=flops, bytes_accessed=moved, transcendentals=0),
    )


def swap(block, axis, size, distance):
    return lax.ppermute(block, axis, [(s, s ^ distance) for s in range(size)])


def gather_pairs(block, axis, size):
    have, blocks = PAIR, [block]
    while have < size:
        if have > PAIR:
            shape = (len(blocks) * block.shape[0], block.shape[1])
            block = call(join_kernel, jax.ShapeDtypeStruct(shape, block.dtype), [VMEM] * len(blocks))(*blocks)
        radix = min(4, size // have)
        blocks = [swap(block, axis, size, r * have) for r in range(radix - 1, 0, -1)] + [block]
        have *= radix
    return blocks


def per_device(sizes, queries, keys, values, document_lengths, pair_ids):
    replicas, parts = sizes
    tokens, features = queries.shape
    width = features // PAIR
    kv_width = keys.shape[1] // PAIR
    docs = DOCS * replicas
    f32, bf16 = jnp.float32, jnp.bfloat16
    struct = jax.ShapeDtypeStruct
    key_far, query_near = swap(keys, "sp", parts, 2), swap(queries, "sp", parts, 1)
    arguments = [pltpu.with_memory_space_constraint(x, pltpu.HBM) for x in (pair_ids, queries, keys, values)]
    query_own, key_own, value_own, value_send, near, bias, of_doc, partner = call(
        functools.partial(plan_kernel, parts),
        (
            struct((tokens, width), bf16),
            *(struct((tokens, kv_width), bf16),) * 3,
            struct((tokens, 2 * kv_width), bf16),
            struct((PAIR * tokens, parts * tokens), f32),
            struct((DOCS, parts * tokens), f32),
            struct((DOCS, docs), f32),
        ),
        [HBM] * 5,
        [
            pltpu.SMEM((1, DOCS), jnp.int32),
            pltpu.SMEM((DOCS,), jnp.int32),
            pltpu.SemaphoreType.DMA((6 * PAIR,)),
            pltpu.SemaphoreType.DMA((2,)),
        ],
        moved=2 * tokens * features + 4 * keys.size,
    )(pltpu.with_memory_space_constraint(document_lengths, pltpu.HBM), *arguments)
    near = swap(near, "sp", parts, 1)
    value_far = swap(value_own, "sp", parts, 2)
    value_last = swap(value_send, "sp", parts, 3)
    last = [
        swap(cut, "sp", parts, 1)
        for cut in call(cut_kernel, (struct((tokens, HEAD_SIZE), bf16),) * PAIR, [VMEM])(key_far)
    ]
    sums = call(
        scores_kernel,
        struct((PAIR * HEAD_GROUP, 1, parts * tokens), f32),
        [VMEM] * 8,
        flops=tokens * features * tokens * parts,
        moved=2 * queries.size + 4 * parts * keys.size,
    )(bias, query_own, query_near, key_own, near, key_far, *last)
    partial, rounded = call(
        values_kernel, (struct((DOCS, width), f32), struct((DOCS, width), bf16)), [VMEM] * 6
    )(sums, of_doc, value_own, near, value_far, value_last)
    corner = swap(rounded, ("dp", "sp"), replicas * parts, parts + 2)
    far = swap(rounded, "sp", parts, 2)
    beside = swap(rounded, "dp", replicas, 1)
    sent = call(pool_kernel, struct((PAIR * DOCS, width), bf16), [VMEM] * 4)(corner, far, beside, partial)
    blocks = gather_pairs(sent, "dp", replicas)
    gram = call(gram_kernel, struct((docs, docs), f32), [VMEM] * len(blocks))(*blocks)
    return call(
        grads_kernel,
        (struct((DOCS, features // parts), bf16), struct((DOCS, features // parts), f32)),
        [VMEM] * (5 + len(blocks)),
    )(partner, gram, swap(gram, "sp", parts, 1), *blocks, partial, far)


def solution(mesh):
    sizes = (mesh.shape["dp"], mesh.shape["sp"])
    return jax.shard_map(
        functools.partial(per_device, sizes),
        mesh=mesh,
        in_specs=(
            P(("dp", "sp"), None),
            P(("dp", "sp"), None),
            P(("dp", "sp"), None),
            P("dp", None),
            P("dp"),
        ),
        out_specs=(P("dp", "sp"), P("dp", "sp")),
        check_vma=False,
    )
```

```python
import functools
import math

import jax
import jax.numpy as jnp
from jax import lax
from jax.experimental import pallas as pl
from jax.experimental.pallas import tpu as pltpu
from jax.sharding import PartitionSpec as P

QUERY_HEADS = 28
KEY_VALUE_HEADS = 4
HEAD_SIZE = 128
HEAD_GROUP = QUERY_HEADS // KEY_VALUE_HEADS
GROUP_WIDTH = HEAD_GROUP * HEAD_SIZE
PAIR = 2
DOCS = 8
SOFTMAX_TEMP = 0.02
VMEM_LIMIT = 48 * 1024 * 1024

VMEM = pl.BlockSpec(memory_space=pltpu.VMEM)
HBM = pl.BlockSpec(memory_space=pltpu.HBM)


def segments(lengths_ref, places):
    end = lengths_ref[0, 0]
    segment = (places >= end).astype(jnp.int32)
    for d in range(1, DOCS):
        end = end + lengths_ref[0, d]
        segment = segment + (places >= end).astype(jnp.int32)
    return segment


def plan_kernel(parts, lengths_hbm, pairs_hbm, q_hbm, k_hbm, v_hbm, *refs):
    q_out, k_out, v_out, near_out, k_far_out, v_far_out, bias_ref, doc_ref, partner_ref, lengths_ref, pairs_ref, sem, small_sem = refs
    span = k_hbm.shape[0]
    me = lax.axis_index("sp")
    core = lax.rem(me, PAIR)
    small = [
        pltpu.make_async_copy(lengths_hbm, lengths_ref, small_sem.at[0]),
        pltpu.make_async_copy(pairs_hbm, pairs_ref, small_sem.at[1]),
    ]
    for copy in small:
        copy.start()
    copies = []

    def cut(source, other, target, start):
        width = source.shape[1] // KEY_VALUE_HEADS
        for p in range(PAIR):
            first = pl.multiple_of((PAIR * p + (core ^ other)) * width, HEAD_SIZE)
            copies.append(
                pltpu.make_async_copy(
                    source.at[:, pl.ds(first, width)],
                    target.at[:, start + p * width : start + (p + 1) * width],
                    sem.at[len(copies)],
                )
            )

    pair_width = PAIR * HEAD_SIZE
    cut(k_hbm, 0, k_out, 0)
    cut(k_hbm, 1, k_far_out, 0)
    cut(k_hbm, 1, near_out, PAIR * GROUP_WIDTH)
    cut(q_hbm, 1, near_out, 0)
    cut(v_hbm, 1, near_out, PAIR * GROUP_WIDTH + pair_width)
    cut(v_hbm, 0, v_out, 0)
    cut(v_hbm, 1, v_far_out, 0)
    cut(q_hbm, 0, q_out, 0)
    for copy in copies:
        copy.start()
    for copy in small:
        copy.wait()
    doc = lax.broadcasted_iota(jnp.int32, (DOCS, span), 0)
    weight = jnp.zeros((DOCS, span), jnp.float32)
    for d in range(DOCS):
        weight = jnp.where(doc == d, 1.0 / lengths_ref[0, d].astype(jnp.float32), weight)
    row_segments = [
        segments(lengths_ref, (me ^ r) * span + lax.broadcasted_iota(jnp.int32, (span, 1), 0)) for r in range(PAIR)
    ]
    for r in range(parts):
        columns = slice(r * span, (r + 1) * span)
        key_segment = segments(lengths_ref, (me ^ r) * span + lax.broadcasted_iota(jnp.int32, (1, span), 1))
        for t in range(PAIR):
            bias_ref[t * span : (t + 1) * span, columns] = jnp.where(row_segments[t] == key_segment, 0.0, -1e30)
        doc_ref[:, columns] = jnp.where(key_segment == doc, weight, 0.0)
    own = lax.axis_index("dp")
    own_row = lax.broadcasted_iota(jnp.int32, partner_ref.shape, 0)
    own_column = lax.broadcasted_iota(jnp.int32, partner_ref.shape, 1)
    place = jnp.zeros(partner_ref.shape, jnp.int32)
    for d in range(DOCS):
        pair = pairs_ref[d]
        far = (pair // DOCS) ^ own
        block = PAIR * ((far & 1) + 2 * (far >> 2)) + ((far >> 1) & 1)
        place = jnp.where(own_row == d, block * DOCS + lax.rem(pair, DOCS), place)
    partner_ref[...] = jnp.where(own_column == place, 2.0, 0.0)
    for copy in copies:
        copy.wait()


def scores_kernel(bias_ref, q_own, k_own, near, k_far, k_last, sums_ref):
    scale = HEAD_SIZE ** (-0.5) * math.log2(math.e)
    for p in range(PAIR):
        here = slice(p * HEAD_SIZE, (p + 1) * HEAD_SIZE)
        beside = PAIR * GROUP_WIDTH + p * HEAD_SIZE
        key_head = jnp.concatenate(
            [k_own[:, here], near[:, beside : beside + HEAD_SIZE], k_far[:, here], k_last[:, here]], axis=0
        )
        for h in range(HEAD_GROUP):
            place = (p * HEAD_GROUP + h) * HEAD_SIZE
            total = None
            for t, q_ref in enumerate((q_own, near)):
                query = q_ref[:, place : place + HEAD_SIZE]
                rows = query.shape[0]
                scores = lax.dot_general(
                    query, key_head, (((1,), (1,)), ((), ())), preferred_element_type=jnp.float32
                )
                scores = scores + bias_ref[t * rows : (t + 1) * rows]
                largest = jnp.max(scores, axis=1, keepdims=True)
                weights = jnp.exp2((scores - largest) * scale)
                probs = weights * (1.0 / jnp.sum(weights, axis=1, keepdims=True))
                summed = jnp.sum(probs, axis=0, keepdims=True)
                total = summed if total is None else total + summed
            row = p * HEAD_GROUP + h
            sums_ref[row : row + 1] = total


def values_kernel(sums_ref, doc_ref, v_own, near, v_far, v_last, out_ref, sent_ref):
    for p in range(PAIR):
        here = slice(p * HEAD_SIZE, (p + 1) * HEAD_SIZE)
        beside = PAIR * (GROUP_WIDTH + HEAD_SIZE) + p * HEAD_SIZE
        value_head = jnp.concatenate(
            [v_own[:, here], near[:, beside : beside + HEAD_SIZE], v_far[:, here], v_last[:, here]], axis=0
        )
        rows = range(p * HEAD_GROUP, (p + 1) * HEAD_GROUP)
        spread = jnp.concatenate([sums_ref[row : row + 1] * doc_ref[...] for row in rows], axis=0)
        high = spread.astype(jnp.bfloat16)
        low = (spread - high.astype(jnp.float32)).astype(jnp.bfloat16)
        summed = jnp.dot(high, value_head, preferred_element_type=jnp.float32) + jnp.dot(
            low, value_head, preferred_element_type=jnp.float32
        )
        for h, row in enumerate(rows):
            out_ref[:, row * HEAD_SIZE : (row + 1) * HEAD_SIZE] = summed[h * DOCS : (h + 1) * DOCS]
    sent_ref[...] = out_ref[...].astype(jnp.bfloat16)


def pool_kernel(corner_ref, far_ref, next_ref, own_ref, sent_ref):
    pooled = own_ref[...] + far_ref[...].astype(jnp.float32)
    beside = next_ref[...].astype(jnp.float32) + corner_ref[...].astype(jnp.float32)
    sent_ref[...] = jnp.concatenate([pooled, beside], axis=0).astype(jnp.bfloat16)


def in_order(refs):
    return (refs[-1], *refs[-3::-1], refs[-2])


def join_kernel(*refs):
    refs[-1][...] = jnp.concatenate([ref[...] for ref in in_order(refs[:-1])], axis=0)


def gram_kernel(*refs):
    every = jnp.concatenate([ref[...] for ref in in_order(refs[:-1])], axis=0)
    refs[-1][...] = lax.dot_general(every, every, (((1,), (1,)), ((), ())), preferred_element_type=jnp.float32)


def grads_kernel(partner_ref, gram_one, gram_two, *refs):
    every_refs, (own_ref, far_ref, emb_ref, grads_ref) = refs[:-4], refs[-4:]
    gram = gram_one[...] + gram_two[...]
    docs = gram.shape[0]
    columns = pl.ds(pl.multiple_of((lax.axis_index("sp") // PAIR) * GROUP_WIDTH, HEAD_SIZE), GROUP_WIDTH)
    row = lax.broadcasted_iota(jnp.int32, (docs, docs), 0)
    column = lax.broadcasted_iota(jnp.int32, (docs, docs), 1)
    diagonal = row == column
    square = jnp.where(diagonal, gram, 0.0)
    inverse_column = lax.rsqrt(jnp.sum(square, axis=1, keepdims=True) + 1e-6)
    inverse_row = lax.rsqrt(jnp.sum(square, axis=0, keepdims=True) + 1e-6)
    cosine = gram * inverse_column * inverse_row
    weights = jnp.where(diagonal, 0.0, jnp.exp(cosine * (1.0 / SOFTMAX_TEMP)))
    own = weights[:DOCS]
    total = 1.0 / jnp.sum(own, axis=1, keepdims=True) + 1.0 / jnp.sum(weights, axis=0, keepdims=True)
    both = own * total - partner_ref[...]
    along = jnp.sum(both * cosine[:DOCS], axis=1, keepdims=True) * (1.0 / SOFTMAX_TEMP)
    weighted = both * inverse_row * (1.0 / SOFTMAX_TEMP)
    high = weighted.astype(jnp.bfloat16)
    low = (weighted - high.astype(jnp.float32)).astype(jnp.bfloat16)
    every = jnp.concatenate([ref[:, columns] for ref in in_order(every_refs)], axis=0)
    gradient = jnp.dot(high, every, preferred_element_type=jnp.float32) + jnp.dot(
        low, every, preferred_element_type=jnp.float32
    )
    inverse = inverse_column[:DOCS]
    pooled = own_ref[:, columns] + far_ref[:, columns].astype(jnp.float32)
    embeddings = (pooled * inverse).astype(jnp.bfloat16)
    emb_ref[...] = embeddings
    grads_ref[...] = (gradient - embeddings.astype(jnp.float32) * along) * inverse


def call(kernel, out_shape, in_specs, scratch_shapes=(), flops=0, moved=0):
    return pl.pallas_call(
        kernel,
        out_shape=out_shape,
        in_specs=in_specs,
        out_specs=jax.tree.map(lambda _: VMEM, out_shape),
        scratch_shapes=scratch_shapes,
        compiler_params=pltpu.CompilerParams(vmem_limit_bytes=VMEM_LIMIT),
        cost_estimate=pl.CostEstimate(flops=flops, bytes_accessed=moved, transcendentals=0),
    )


def swap(block, axis, size, distance):
    return lax.ppermute(block, axis, [(s, s ^ distance) for s in range(size)])


def gather_pairs(block, axis, size):
    strides, blocks = [1] + [1 << i for i in range(2, size.bit_length() - 1)], [block]
    while strides:
        if len(blocks) > 1:
            shape = (len(blocks) * block.shape[0], block.shape[1])
            block = call(join_kernel, jax.ShapeDtypeStruct(shape, block.dtype), [VMEM] * len(blocks))(*blocks)
        low, high, strides = strides[0], sum(strides[1:2]), strides[2:]
        distances = [low, high, low + high] if high else [low]
        blocks = [swap(block, axis, size, r) for r in (*distances[-2::-1], distances[-1])] + [block]
    return blocks


def per_device(sizes, queries, keys, values, document_lengths, pair_ids):
    replicas, parts = sizes
    tokens, features = queries.shape
    width = features // PAIR
    kv_width = keys.shape[1] // PAIR
    docs = DOCS * replicas
    f32, bf16 = jnp.float32, jnp.bfloat16
    struct = jax.ShapeDtypeStruct
    query_own, key_own, value_own, near, key_send, value_send, bias, of_doc, partner = call(
        functools.partial(plan_kernel, parts),
        (
            struct((tokens, width), bf16),
            struct((tokens, kv_width), bf16),
            struct((tokens, kv_width), bf16),
            struct((tokens, width + 2 * kv_width), bf16),
            struct((tokens, kv_width), bf16),
            struct((tokens, kv_width), bf16),
            struct((PAIR * tokens, parts * tokens), f32),
            struct((DOCS, parts * tokens), f32),
            struct((DOCS, docs), f32),
        ),
        [HBM] * 5,
        [
            pltpu.SMEM((1, DOCS), jnp.int32),
            pltpu.SMEM((DOCS,), jnp.int32),
            pltpu.SemaphoreType.DMA((8 * PAIR,)),
            pltpu.SemaphoreType.DMA((2,)),
        ],
        moved=2 * tokens * features + 4 * keys.size,
    )(*(pltpu.with_memory_space_constraint(x, pltpu.HBM) for x in (document_lengths, pair_ids, queries, keys, values)))
    near = swap(near, "sp", parts, 1)
    value_far = swap(value_own, "sp", parts, 2)
    value_last = swap(value_send, "sp", parts, 3)
    key_far = swap(key_own, "sp", parts, 2)
    key_last = swap(key_send, "sp", parts, 3)
    sums = call(
        scores_kernel,
        struct((PAIR * HEAD_GROUP, parts * tokens), f32),
        [VMEM] * 6,
        flops=tokens * features * tokens * parts,
        moved=2 * queries.size + 4 * parts * keys.size,
    )(bias, query_own, key_own, near, key_far, key_last)
    partial, rounded = call(
        values_kernel, (struct((DOCS, width), f32), struct((DOCS, width), bf16)), [VMEM] * 6
    )(sums, of_doc, value_own, near, value_far, value_last)
    corner = swap(rounded, ("dp", "sp"), replicas * parts, 2 * parts + 2)
    far = swap(rounded, "sp", parts, 2)
    beside = swap(rounded, "dp", replicas, 2)
    sent = call(pool_kernel, struct((PAIR * DOCS, width), bf16), [VMEM] * 4)(corner, far, beside, partial)
    blocks = gather_pairs(sent, "dp", replicas)
    gram = call(gram_kernel, struct((docs, docs), f32), [VMEM] * len(blocks))(*blocks)
    return call(
        grads_kernel,
        (struct((DOCS, features // parts), bf16), struct((DOCS, features // parts), f32)),
        [VMEM] * (5 + len(blocks)),
    )(partner, gram, swap(gram, "sp", parts, 1), *blocks, partial, far)


def solution(mesh):
    sizes = (mesh.shape["dp"], mesh.shape["sp"])
    return jax.shard_map(
        functools.partial(per_device, sizes),
        mesh=mesh,
        in_specs=(
            P(("dp", "sp"), None),
            P(("dp", "sp"), None),
            P(("dp", "sp"), None),
            P("dp", None),
            P("dp"),
        ),
        out_specs=(P("dp", "sp"), P("dp", "sp")),
        check_vma=False,
    )
```

```python
import functools
import math

import jax
import jax.numpy as jnp
from jax import lax
from jax.experimental import pallas as pl
from jax.experimental.pallas import tpu as pltpu
from jax.sharding import PartitionSpec as P

QUERY_HEADS = 28
KEY_VALUE_HEADS = 4
HEAD_SIZE = 128
HEAD_GROUP = QUERY_HEADS // KEY_VALUE_HEADS
GROUP_WIDTH = HEAD_GROUP * HEAD_SIZE
PAIR = 2
DOCS = 8
SOFTMAX_TEMP = 0.02
VMEM_LIMIT = 48 * 1024 * 1024

VMEM = pl.BlockSpec(memory_space=pltpu.VMEM)
HBM = pl.BlockSpec(memory_space=pltpu.HBM)


def segments(lengths_ref, places):
    end = lengths_ref[0, 0]
    segment = (places >= end).astype(jnp.int32)
    for d in range(1, DOCS):
        end = end + lengths_ref[0, d]
        segment = segment + (places >= end).astype(jnp.int32)
    return segment


def group_columns(ref, group):
    width = ref.shape[1] // KEY_VALUE_HEADS
    return ref.at[:, pl.ds(pl.multiple_of(group * width, HEAD_SIZE), width)]


def cut_kernel(q_hbm, k_hbm, v_hbm, k_out, v_out, near_out, k_far_out, v_far_out, sem):
    core = lax.rem(lax.axis_index("sp"), PAIR)
    near_k, near_v = PAIR * GROUP_WIDTH, PAIR * (GROUP_WIDTH + HEAD_SIZE)
    plans = [(k_hbm, 0, k_out, 0), (k_hbm, 1, k_far_out, 0), (q_hbm, 1, near_out, 0), (k_hbm, 1, near_out, near_k)]
    plans += [(v_hbm, 1, near_out, near_v), (v_hbm, 0, v_out, 0), (v_hbm, 1, v_far_out, 0)]
    copies = []
    for source, other, target, start in plans:
        width = source.shape[1] // KEY_VALUE_HEADS
        for p in range(PAIR):
            copies.append(
                pltpu.make_async_copy(
                    group_columns(source, PAIR * p + (core ^ other)),
                    target.at[:, start + p * width : start + (p + 1) * width],
                    sem.at[len(copies)],
                )
            )
    for copy in copies:
        copy.start()
    for copy in copies:
        copy.wait()


def plan_kernel(parts, lengths_hbm, pairs_hbm, q_hbm, q_out, bias_ref, doc_ref, partner_ref, lengths_ref, pairs_ref, sem):
    span = q_hbm.shape[0]
    me = lax.axis_index("sp")
    core = lax.rem(me, PAIR)
    small = [
        pltpu.make_async_copy(lengths_hbm, lengths_ref, sem.at[PAIR]),
        pltpu.make_async_copy(pairs_hbm, pairs_ref, sem.at[PAIR + 1]),
    ]
    copies = [
        pltpu.make_async_copy(
            group_columns(q_hbm, PAIR * p + core),
            q_out.at[:, p * GROUP_WIDTH : (p + 1) * GROUP_WIDTH],
            sem.at[p],
        )
        for p in range(PAIR)
    ]
    for copy in small + copies:
        copy.start()
    for copy in small:
        copy.wait()
    doc = lax.broadcasted_iota(jnp.int32, (DOCS, span), 0)
    weight = jnp.zeros((DOCS, span), jnp.float32)
    for d in range(DOCS):
        weight = jnp.where(doc == d, 1.0 / lengths_ref[0, d].astype(jnp.float32), weight)
    row_segments = [
        segments(lengths_ref, (me ^ r) * span + lax.broadcasted_iota(jnp.int32, (span, 1), 0)) for r in range(PAIR)
    ]
    for r in range(parts):
        columns = slice(r * span, (r + 1) * span)
        key_segment = segments(lengths_ref, (me ^ r) * span + lax.broadcasted_iota(jnp.int32, (1, span), 1))
        for t in range(PAIR):
            bias_ref[t * span : (t + 1) * span, columns] = jnp.where(row_segments[t] == key_segment, 0.0, -1e30)
        doc_ref[:, columns] = jnp.where(key_segment == doc, weight, 0.0)
    own = lax.axis_index("dp")
    own_row = lax.broadcasted_iota(jnp.int32, partner_ref.shape, 0)
    own_column = lax.broadcasted_iota(jnp.int32, partner_ref.shape, 1)
    place = jnp.zeros(partner_ref.shape, jnp.int32)
    for d in range(DOCS):
        pair = pairs_ref[d]
        place = jnp.where(own_row == d, ((pair // DOCS) ^ own) * DOCS + lax.rem(pair, DOCS), place)
    partner_ref[...] = jnp.where(own_column == place, 2.0, 0.0)
    for copy in copies:
        copy.wait()


def scores_kernel(bias_ref, q_own, k_own, near, k_far, k_last, sums_ref):
    scale = HEAD_SIZE ** (-0.5) * math.log2(math.e)
    for p in range(PAIR):
        here = slice(p * HEAD_SIZE, (p + 1) * HEAD_SIZE)
        beside = PAIR * GROUP_WIDTH + p * HEAD_SIZE
        key_head = jnp.concatenate(
            [k_own[:, here], near[:, beside : beside + HEAD_SIZE], k_far[:, here], k_last[:, here]], axis=0
        )
        for h in range(HEAD_GROUP):
            place = (p * HEAD_GROUP + h) * HEAD_SIZE
            total = None
            for t, q_ref in enumerate((q_own, near)):
                query = q_ref[:, place : place + HEAD_SIZE]
                rows = query.shape[0]
                scores = lax.dot_general(
                    query, key_head, (((1,), (1,)), ((), ())), preferred_element_type=jnp.float32
                )
                scores = scores + bias_ref[t * rows : (t + 1) * rows]
                largest = jnp.max(scores, axis=1, keepdims=True)
                weights = jnp.exp2((scores - largest) * scale)
                probs = weights * (1.0 / jnp.sum(weights, axis=1, keepdims=True))
                summed = jnp.sum(probs, axis=0, keepdims=True)
                total = summed if total is None else total + summed
            row = p * HEAD_GROUP + h
            sums_ref[row : row + 1] = total


def values_kernel(sums_ref, doc_ref, v_own, near, v_far, v_last, out_ref, sent_ref):
    for p in range(PAIR):
        here = slice(p * HEAD_SIZE, (p + 1) * HEAD_SIZE)
        beside = PAIR * (GROUP_WIDTH + HEAD_SIZE) + p * HEAD_SIZE
        value_head = jnp.concatenate(
            [v_own[:, here], near[:, beside : beside + HEAD_SIZE], v_far[:, here], v_last[:, here]], axis=0
        )
        rows = range(p * HEAD_GROUP, (p + 1) * HEAD_GROUP)
        spread = jnp.concatenate([sums_ref[row : row + 1] * doc_ref[...] for row in rows], axis=0)
        high = spread.astype(jnp.bfloat16)
        low = (spread - high.astype(jnp.float32)).astype(jnp.bfloat16)
        summed = jnp.dot(high, value_head, preferred_element_type=jnp.float32) + jnp.dot(
            low, value_head, preferred_element_type=jnp.float32
        )
        for h, row in enumerate(rows):
            out_ref[:, row * HEAD_SIZE : (row + 1) * HEAD_SIZE] = summed[h * DOCS : (h + 1) * DOCS]
    sent_ref[...] = out_ref[...].astype(jnp.bfloat16)


def pool_kernel(corner_ref, far_ref, next_ref, own_ref, sent_ref):
    pooled = own_ref[...] + far_ref[...].astype(jnp.float32)
    beside = next_ref[...].astype(jnp.float32) + corner_ref[...].astype(jnp.float32)
    sent_ref[...] = jnp.concatenate([pooled, beside], axis=0).astype(jnp.bfloat16)


def in_order(refs):
    return (refs[-1], *refs[-3::-1], refs[-2])


def join_kernel(*refs):
    refs[-1][...] = jnp.concatenate([ref[...] for ref in in_order(refs[:-1])], axis=0)


def gram_kernel(*refs):
    every = jnp.concatenate([ref[...] for ref in in_order(refs[:-1])], axis=0)
    refs[-1][...] = lax.dot_general(every, every, (((1,), (1,)), ((), ())), preferred_element_type=jnp.float32)


def grads_kernel(partner_ref, gram_one, gram_two, *refs):
    every_refs, (own_ref, far_ref, emb_ref, grads_ref) = refs[:-4], refs[-4:]
    gram = gram_one[...] + gram_two[...]
    docs = gram.shape[0]
    columns = pl.ds(pl.multiple_of((lax.axis_index("sp") // PAIR) * GROUP_WIDTH, HEAD_SIZE), GROUP_WIDTH)
    row = lax.broadcasted_iota(jnp.int32, (docs, docs), 0)
    column = lax.broadcasted_iota(jnp.int32, (docs, docs), 1)
    diagonal = row == column
    square = jnp.where(diagonal, gram, 0.0)
    inverse_column = lax.rsqrt(jnp.sum(square, axis=1, keepdims=True) + 1e-6)
    inverse_row = lax.rsqrt(jnp.sum(square, axis=0, keepdims=True) + 1e-6)
    cosine = gram * inverse_column * inverse_row
    logits = jnp.where(diagonal, -jnp.inf, cosine * (1.0 / SOFTMAX_TEMP))
    own = logits[:DOCS]
    largest = jnp.max(own, axis=1, keepdims=True)
    weights = jnp.exp(own - largest)
    probs = weights / jnp.sum(weights, axis=1, keepdims=True)
    largest_row = jnp.max(logits, axis=0, keepdims=True)
    total_row = jnp.sum(jnp.exp(logits - largest_row), axis=0, keepdims=True)
    probs = probs + jnp.exp(own - largest_row) / total_row
    both = probs - partner_ref[...]
    along = jnp.sum(both * cosine[:DOCS], axis=1, keepdims=True) * (1.0 / SOFTMAX_TEMP)
    weighted = both * inverse_row * (1.0 / SOFTMAX_TEMP)
    high = weighted.astype(jnp.bfloat16)
    low = (weighted - high.astype(jnp.float32)).astype(jnp.bfloat16)
    every = jnp.concatenate([ref[:, columns] for ref in in_order(every_refs)], axis=0)
    gradient = jnp.dot(high, every, preferred_element_type=jnp.float32) + jnp.dot(
        low, every, preferred_element_type=jnp.float32
    )
    inverse = inverse_column[:DOCS]
    pooled = own_ref[:, columns] + far_ref[:, columns].astype(jnp.float32)
    embeddings = (pooled * inverse).astype(jnp.bfloat16)
    emb_ref[...] = embeddings
    grads_ref[...] = (gradient - embeddings.astype(jnp.float32) * along) * inverse


def call(kernel, out_shape, in_specs, scratch_shapes=(), flops=0, moved=0):
    return pl.pallas_call(
        kernel,
        out_shape=out_shape,
        in_specs=in_specs,
        out_specs=jax.tree.map(lambda _: VMEM, out_shape),
        scratch_shapes=scratch_shapes,
        compiler_params=pltpu.CompilerParams(vmem_limit_bytes=VMEM_LIMIT),
        cost_estimate=pl.CostEstimate(flops=flops, bytes_accessed=moved, transcendentals=0),
    )


def swap(block, axis, size, distance):
    return lax.ppermute(block, axis, [(s, s ^ distance) for s in range(size)])


def gather_pairs(block, axis, size):
    have, blocks = PAIR, [block]
    while have < size:
        if have > PAIR:
            shape = (len(blocks) * block.shape[0], block.shape[1])
            block = call(join_kernel, jax.ShapeDtypeStruct(shape, block.dtype), [VMEM] * len(blocks))(*blocks)
        radix = min(4, size // have)
        blocks = [swap(block, axis, size, r * have) for r in (*range(radix - 2, 0, -1), radix - 1)] + [block]
        have *= radix
    return blocks


def per_device(sizes, queries, keys, values, document_lengths, pair_ids):
    replicas, parts = sizes
    tokens, features = queries.shape
    width = features // PAIR
    kv_width = keys.shape[1] // PAIR
    docs = DOCS * replicas
    f32, bf16 = jnp.float32, jnp.bfloat16
    struct = jax.ShapeDtypeStruct
    near_cut = struct((tokens, kv_width), bf16)
    arguments = [pltpu.with_memory_space_constraint(x, pltpu.HBM) for x in (document_lengths, pair_ids, queries, keys, values)]
    key_own, value_own, near, key_send, value_send = call(
        cut_kernel,
        (near_cut, near_cut, struct((tokens, width + 2 * kv_width), bf16), near_cut, near_cut),
        [HBM] * 3,
        [pltpu.SemaphoreType.DMA((7 * PAIR,))],
        moved=tokens * features + 8 * keys.size,
    )(*arguments[2:])
    query_own, bias, of_doc, partner = call(
        functools.partial(plan_kernel, parts),
        (
            struct((tokens, width), bf16),
            struct((PAIR * tokens, parts * tokens), f32),
            struct((DOCS, parts * tokens), f32),
            struct((DOCS, docs), f32),
        ),
        [HBM] * 3,
        [
            pltpu.SMEM((1, DOCS), jnp.int32),
            pltpu.SMEM((DOCS,), jnp.int32),
            pltpu.SemaphoreType.DMA((PAIR + 2,)),
        ],
        moved=2 * tokens * features,
    )(*arguments[:3])
    near = swap(near, "sp", parts, 1)
    value_far = swap(value_own, "sp", parts, 2)
    value_last = swap(value_send, "sp", parts, 3)
    key_far = swap(key_own, "sp", parts, 2)
    key_last = swap(key_send, "sp", parts, 3)
    sums = call(
        scores_kernel,
        struct((PAIR * HEAD_GROUP, parts * tokens), f32),
        [VMEM] * 6,
        flops=tokens * features * tokens * parts,
        moved=2 * queries.size + 4 * parts * keys.size,
    )(bias, query_own, key_own, near, key_far, key_last)
    partial, rounded = call(
        values_kernel, (struct((DOCS, width), f32), struct((DOCS, width), bf16)), [VMEM] * 6
    )(sums, of_doc, value_own, near, value_far, value_last)
    corner = swap(rounded, ("dp", "sp"), replicas * parts, parts + 2)
    far = swap(rounded, "sp", parts, 2)
    beside = swap(rounded, "dp", replicas, 1)
    sent = call(pool_kernel, struct((PAIR * DOCS, width), bf16), [VMEM] * 4)(corner, far, beside, partial)
    blocks = gather_pairs(sent, "dp", replicas)
    gram = call(gram_kernel, struct((docs, docs), f32), [VMEM] * len(blocks))(*blocks)
    return call(
        grads_kernel,
        (struct((DOCS, features // parts), bf16), struct((DOCS, features // parts), f32)),
        [VMEM] * (5 + len(blocks)),
    )(partner, gram, swap(gram, "sp", parts, 1), *blocks, partial, far)


def solution(mesh):
    sizes = (mesh.shape["dp"], mesh.shape["sp"])
    return jax.shard_map(
        functools.partial(per_device, sizes),
        mesh=mesh,
        in_specs=(
            P(("dp", "sp"), None),
            P(("dp", "sp"), None),
            P(("dp", "sp"), None),
            P("dp", None),
            P("dp"),
        ),
        out_specs=(P("dp", "sp"), P("dp", "sp")),
        check_vma=False,
    )
```

```python
import functools
import math

import jax
import jax.numpy as jnp
from jax import lax
from jax.experimental import pallas as pl
from jax.experimental.pallas import tpu as pltpu
from jax.sharding import PartitionSpec as P

QUERY_HEADS = 28
KEY_VALUE_HEADS = 4
HEAD_SIZE = 128
HEAD_GROUP = QUERY_HEADS // KEY_VALUE_HEADS
GROUP_WIDTH = HEAD_GROUP * HEAD_SIZE
PAIR = 2
DOCS = 8
SOFTMAX_TEMP = 0.02
VMEM_LIMIT = 48 * 1024 * 1024

VMEM = pl.BlockSpec(memory_space=pltpu.VMEM)
HBM = pl.BlockSpec(memory_space=pltpu.HBM)


def segments(lengths_ref, places):
    end = lengths_ref[0, 0]
    segment = (places >= end).astype(jnp.int32)
    for d in range(1, DOCS):
        end = end + lengths_ref[0, d]
        segment = segment + (places >= end).astype(jnp.int32)
    return segment


def group_columns(ref, group):
    width = ref.shape[1] // KEY_VALUE_HEADS
    return ref.at[:, pl.ds(pl.multiple_of(group * width, HEAD_SIZE), width)]


def cut_kernel(q_hbm, k_hbm, v_hbm, k_out, v_out, near_out, k_far_out, v_far_out, sem):
    core = lax.rem(lax.axis_index("sp"), PAIR)
    near_k, near_v = PAIR * GROUP_WIDTH, PAIR * (GROUP_WIDTH + HEAD_SIZE)
    plans = [(k_hbm, 0, k_out, 0), (k_hbm, 1, k_far_out, 0), (q_hbm, 1, near_out, 0), (k_hbm, 1, near_out, near_k)]
    plans += [(v_hbm, 1, near_out, near_v), (v_hbm, 0, v_out, 0), (v_hbm, 1, v_far_out, 0)]
    copies = []
    for source, other, target, start in plans:
        width = source.shape[1] // KEY_VALUE_HEADS
        for p in range(PAIR):
            copies.append(
                pltpu.make_async_copy(
                    group_columns(source, PAIR * p + (core ^ other)),
                    target.at[:, start + p * width : start + (p + 1) * width],
                    sem.at[len(copies)],
                )
            )
    for copy in copies:
        copy.start()
    for copy in copies:
        copy.wait()


def plan_kernel(parts, lengths_hbm, pairs_hbm, q_hbm, q_out, bias_ref, doc_ref, partner_ref, lengths_ref, pairs_ref, sem):
    span = q_hbm.shape[0]
    me = lax.axis_index("sp")
    core = lax.rem(me, PAIR)
    small = [
        pltpu.make_async_copy(lengths_hbm, lengths_ref, sem.at[PAIR]),
        pltpu.make_async_copy(pairs_hbm, pairs_ref, sem.at[PAIR + 1]),
    ]
    copies = [
        pltpu.make_async_copy(
            group_columns(q_hbm, PAIR * p + core),
            q_out.at[:, p * GROUP_WIDTH : (p + 1) * GROUP_WIDTH],
            sem.at[p],
        )
        for p in range(PAIR)
    ]
    for copy in small + copies:
        copy.start()
    for copy in small:
        copy.wait()
    doc = lax.broadcasted_iota(jnp.int32, (DOCS, span), 0)
    weight = jnp.zeros((DOCS, span), jnp.float32)
    for d in range(DOCS):
        weight = jnp.where(doc == d, 1.0 / lengths_ref[0, d].astype(jnp.float32), weight)
    row_segments = [
        segments(lengths_ref, (me ^ r) * span + lax.broadcasted_iota(jnp.int32, (span, 1), 0)) for r in range(PAIR)
    ]
    for r in range(parts):
        columns = slice(r * span, (r + 1) * span)
        key_segment = segments(lengths_ref, (me ^ r) * span + lax.broadcasted_iota(jnp.int32, (1, span), 1))
        for t in range(PAIR):
            bias_ref[t * span : (t + 1) * span, columns] = jnp.where(row_segments[t] == key_segment, 0.0, -1e30)
        doc_ref[:, columns] = jnp.where(key_segment == doc, weight, 0.0)
    own = lax.axis_index("dp")
    own_row = lax.broadcasted_iota(jnp.int32, partner_ref.shape, 0)
    own_column = lax.broadcasted_iota(jnp.int32, partner_ref.shape, 1)
    place = jnp.zeros(partner_ref.shape, jnp.int32)
    for d in range(DOCS):
        pair = pairs_ref[d]
        place = jnp.where(own_row == d, ((pair // DOCS) ^ own) * DOCS + lax.rem(pair, DOCS), place)
    partner_ref[...] = jnp.where(own_column == place, 2.0, 0.0)
    for copy in copies:
        copy.wait()


def scores_kernel(bias_ref, q_own, k_own, near, k_far, k_last, sums_ref):
    scale = HEAD_SIZE ** (-0.5) * math.log2(math.e)
    for p in range(PAIR):
        here = slice(p * HEAD_SIZE, (p + 1) * HEAD_SIZE)
        beside = PAIR * GROUP_WIDTH + p * HEAD_SIZE
        key_head = jnp.concatenate(
            [k_own[:, here], near[:, beside : beside + HEAD_SIZE], k_far[:, here], k_last[:, here]], axis=0
        )
        for h in range(HEAD_GROUP):
            place = (p * HEAD_GROUP + h) * HEAD_SIZE
            total = None
            for t, q_ref in enumerate((q_own, near)):
                query = q_ref[:, place : place + HEAD_SIZE]
                rows = query.shape[0]
                scores = lax.dot_general(
                    query, key_head, (((1,), (1,)), ((), ())), preferred_element_type=jnp.float32
                )
                scores = scores + bias_ref[t * rows : (t + 1) * rows]
                largest = jnp.max(scores, axis=1, keepdims=True)
                weights = jnp.exp2((scores - largest) * scale)
                probs = weights * (1.0 / jnp.sum(weights, axis=1, keepdims=True))
                summed = jnp.sum(probs, axis=0, keepdims=True)
                total = summed if total is None else total + summed
            row = p * HEAD_GROUP + h
            sums_ref[row : row + 1] = total


def values_kernel(sums_ref, doc_ref, v_own, near, v_far, v_last, out_ref, sent_ref):
    for p in range(PAIR):
        here = slice(p * HEAD_SIZE, (p + 1) * HEAD_SIZE)
        beside = PAIR * (GROUP_WIDTH + HEAD_SIZE) + p * HEAD_SIZE
        value_head = jnp.concatenate(
            [v_own[:, here], near[:, beside : beside + HEAD_SIZE], v_far[:, here], v_last[:, here]], axis=0
        )
        rows = range(p * HEAD_GROUP, (p + 1) * HEAD_GROUP)
        spread = jnp.concatenate([sums_ref[row : row + 1] * doc_ref[...] for row in rows], axis=0)
        high = spread.astype(jnp.bfloat16)
        low = (spread - high.astype(jnp.float32)).astype(jnp.bfloat16)
        summed = jnp.dot(high, value_head, preferred_element_type=jnp.float32) + jnp.dot(
            low, value_head, preferred_element_type=jnp.float32
        )
        for h, row in enumerate(rows):
            out_ref[:, row * HEAD_SIZE : (row + 1) * HEAD_SIZE] = summed[h * DOCS : (h + 1) * DOCS]
    sent_ref[...] = out_ref[...].astype(jnp.bfloat16)


def pool_kernel(corner_ref, far_ref, next_ref, own_ref, sent_ref):
    pooled = own_ref[...] + far_ref[...].astype(jnp.float32)
    beside = next_ref[...].astype(jnp.float32) + corner_ref[...].astype(jnp.float32)
    sent_ref[...] = jnp.concatenate([pooled, beside], axis=0).astype(jnp.bfloat16)


def in_order(refs):
    return (refs[-1], *refs[-3::-1], refs[-2])


def join_kernel(*refs):
    refs[-1][...] = jnp.concatenate([ref[...] for ref in in_order(refs[:-1])], axis=0)


def gram_kernel(*refs):
    every = jnp.concatenate([ref[...] for ref in in_order(refs[:-1])], axis=0)
    refs[-1][...] = lax.dot_general(every, every, (((1,), (1,)), ((), ())), preferred_element_type=jnp.float32)


def grads_kernel(partner_ref, gram_one, gram_two, *refs):
    every_refs, (own_ref, far_ref, emb_ref, grads_ref) = refs[:-4], refs[-4:]
    gram = gram_one[...] + gram_two[...]
    docs = gram.shape[0]
    columns = pl.ds(pl.multiple_of((lax.axis_index("sp") // PAIR) * GROUP_WIDTH, HEAD_SIZE), GROUP_WIDTH)
    row = lax.broadcasted_iota(jnp.int32, (docs, docs), 0)
    column = lax.broadcasted_iota(jnp.int32, (docs, docs), 1)
    diagonal = row == column
    square = jnp.where(diagonal, gram, 0.0)
    inverse_column = lax.rsqrt(jnp.sum(square, axis=1, keepdims=True) + 1e-6)
    inverse_row = lax.rsqrt(jnp.sum(square, axis=0, keepdims=True) + 1e-6)
    cosine = gram * inverse_column * inverse_row
    weights = jnp.where(diagonal, 0.0, jnp.exp(cosine * (1.0 / SOFTMAX_TEMP)))
    own = weights[:DOCS]
    total = 1.0 / jnp.sum(own, axis=1, keepdims=True) + 1.0 / jnp.sum(weights, axis=0, keepdims=True)
    both = own * total - partner_ref[...]
    along = jnp.sum(both * cosine[:DOCS], axis=1, keepdims=True) * (1.0 / SOFTMAX_TEMP)
    weighted = both * inverse_row * (1.0 / SOFTMAX_TEMP)
    high = weighted.astype(jnp.bfloat16)
    low = (weighted - high.astype(jnp.float32)).astype(jnp.bfloat16)
    every = jnp.concatenate([ref[:, columns] for ref in in_order(every_refs)], axis=0)
    gradient = jnp.dot(high, every, preferred_element_type=jnp.float32) + jnp.dot(
        low, every, preferred_element_type=jnp.float32
    )
    inverse = inverse_column[:DOCS]
    pooled = own_ref[:, columns] + far_ref[:, columns].astype(jnp.float32)
    embeddings = (pooled * inverse).astype(jnp.bfloat16)
    emb_ref[...] = embeddings
    grads_ref[...] = (gradient - embeddings.astype(jnp.float32) * along) * inverse


def call(kernel, out_shape, in_specs, scratch_shapes=(), flops=0, moved=0):
    return pl.pallas_call(
        kernel,
        out_shape=out_shape,
        in_specs=in_specs,
        out_specs=jax.tree.map(lambda _: VMEM, out_shape),
        scratch_shapes=scratch_shapes,
        compiler_params=pltpu.CompilerParams(vmem_limit_bytes=VMEM_LIMIT),
        cost_estimate=pl.CostEstimate(flops=flops, bytes_accessed=moved, transcendentals=0),
    )


def swap(block, axis, size, distance):
    return lax.ppermute(block, axis, [(s, s ^ distance) for s in range(size)])


def gather_pairs(block, axis, size):
    have, blocks = PAIR, [block]
    while have < size:
        if have > PAIR:
            shape = (len(blocks) * block.shape[0], block.shape[1])
            block = call(join_kernel, jax.ShapeDtypeStruct(shape, block.dtype), [VMEM] * len(blocks))(*blocks)
        radix = min(4, size // have)
        blocks = [swap(block, axis, size, r * have) for r in (*range(radix - 2, 0, -1), radix - 1)] + [block]
        have *= radix
    return blocks


def per_device(sizes, queries, keys, values, document_lengths, pair_ids):
    replicas, parts = sizes
    tokens, features = queries.shape
    width = features // PAIR
    kv_width = keys.shape[1] // PAIR
    docs = DOCS * replicas
    f32, bf16 = jnp.float32, jnp.bfloat16
    struct = jax.ShapeDtypeStruct
    near_cut = struct((tokens, kv_width), bf16)
    arguments = [pltpu.with_memory_space_constraint(x, pltpu.HBM) for x in (document_lengths, pair_ids, queries, keys, values)]
    key_own, value_own, near, key_send, value_send = call(
        cut_kernel,
        (near_cut, near_cut, struct((tokens, width + 2 * kv_width), bf16), near_cut, near_cut),
        [HBM] * 3,
        [pltpu.SemaphoreType.DMA((7 * PAIR,))],
        moved=tokens * features + 8 * keys.size,
    )(*arguments[2:])
    query_own, bias, of_doc, partner = call(
        functools.partial(plan_kernel, parts),
        (
            struct((tokens, width), bf16),
            struct((PAIR * tokens, parts * tokens), f32),
            struct((DOCS, parts * tokens), f32),
            struct((DOCS, docs), f32),
        ),
        [HBM] * 3,
        [
            pltpu.SMEM((1, DOCS), jnp.int32),
            pltpu.SMEM((DOCS,), jnp.int32),
            pltpu.SemaphoreType.DMA((PAIR + 2,)),
        ],
        moved=2 * tokens * features,
    )(*arguments[:3])
    near = swap(near, "sp", parts, 1)
    value_far = swap(value_own, "sp", parts, 2)
    value_last = swap(value_send, "sp", parts, 3)
    key_far = swap(key_own, "sp", parts, 2)
    key_last = swap(key_send, "sp", parts, 3)
    sums = call(
        scores_kernel,
        struct((PAIR * HEAD_GROUP, parts * tokens), f32),
        [VMEM] * 6,
        flops=tokens * features * tokens * parts,
        moved=2 * queries.size + 4 * parts * keys.size,
    )(bias, query_own, key_own, near, key_far, key_last)
    partial, rounded = call(
        values_kernel, (struct((DOCS, width), f32), struct((DOCS, width), bf16)), [VMEM] * 6
    )(sums, of_doc, value_own, near, value_far, value_last)
    corner = swap(rounded, ("dp", "sp"), replicas * parts, parts + 2)
    far = swap(rounded, "sp", parts, 2)
    beside = swap(rounded, "dp", replicas, 1)
    sent = call(pool_kernel, struct((PAIR * DOCS, width), bf16), [VMEM] * 4)(corner, far, beside, partial)
    blocks = gather_pairs(sent, "dp", replicas)
    gram = call(gram_kernel, struct((docs, docs), f32), [VMEM] * len(blocks))(*blocks)
    return call(
        grads_kernel,
        (struct((DOCS, features // parts), bf16), struct((DOCS, features // parts), f32)),
        [VMEM] * (5 + len(blocks)),
    )(partner, gram, swap(gram, "sp", parts, 1), *blocks, partial, far)


def solution(mesh):
    sizes = (mesh.shape["dp"], mesh.shape["sp"])
    return jax.shard_map(
        functools.partial(per_device, sizes),
        mesh=mesh,
        in_specs=(
            P(("dp", "sp"), None),
            P(("dp", "sp"), None),
            P(("dp", "sp"), None),
            P("dp", None),
            P("dp"),
        ),
        out_specs=(P("dp", "sp"), P("dp", "sp")),
        check_vma=False,
    )
```
